32 devices in a mesh: dp: 4 (over z), row: 4 (over y, core), col: 2 (over x).
Axes of the slice: x: 2, y: 2, z: 4, core: 2. Of those that a mesh axis runs over, the one named last changes fastest.
Arguments:
- latents_in: float32 [8192, 1152], P(('dp', 'col'), 'row'), may hold values from -4 to 4, as said below
- conditioning: float32 [32, 1152], P('dp', 'col'), may hold values from -4 to 4, as said below
- cotangent: float32 [8192, 1152], P(('dp', 'col'), 'row'), may hold values from -4 to 4, as said below
- modulation_weight: float32 [1152, 6, 1152], P('col', None, 'row'), may hold values from -0.11785113 to 0.11785113, as said below
- attention_in: float32 [3, 1152, 1152], P(None, 'row', 'col'), may hold values from -0.11785113 to 0.11785113, as said below
- attention_out: float32 [1152, 1152], P('col', 'row'), may hold values from -0.47140452 to 0.47140452, as said below
- expand_weight: float32 [1152, 4, 1152], P('row', None, 'col'), may hold values from -0.11785113 to 0.11785113, as said below
- contract_weight: float32 [4, 1152, 1152], P(None, 'col', 'row'), may hold values from -0.058925565 to 0.058925565, as said below
- bias_rows: float32 [8, 1152], P(None, 'row'), may hold values from -1.2 to 1.2, as said below
- bias_cols: float32 [6, 1152], P(None, 'col'), may hold values from -1.2 to 1.2, as said below
- first_modulation: float32 [1152, 6, 1152], P('col', None, 'row'), may hold values from -24.256591 to 24.256591, as said below
- first_attention_in: float32 [3, 1152, 1152], P(None, 'row', 'col'), may hold values from -24.256591 to 24.256591, as said below
- first_attention_out: float32 [1152, 1152], P('col', 'row'), may hold values from -24.256591 to 24.256591, as said below
- first_expand: float32 [1152, 4, 1152], P('row', None, 'col'), may hold values from -24.256591 to 24.256591, as said below
- first_contract: float32 [4, 1152, 1152], P(None, 'col', 'row'), may hold values from -24.256591 to 24.256591, as said below
- first_bias_rows: float32 [8, 1152], P(None, 'row'), may hold values from -24.256591 to 24.256591, as said below
- first_bias_cols: float32 [6, 1152], P(None, 'col'), may hold values from -24.256591 to 24.256591, as said below
- second_modulation: float32 [1152, 6, 1152], P('col', None, 'row'), may hold values from 1.47456 to 11.79648
- second_attention_in: float32 [3, 1152, 1152], P(None, 'row', 'col'), may hold values from 1.47456 to 11.79648
- second_attention_out: float32 [1152, 1152], P('col', 'row'), may hold values from 1.47456 to 11.79648
- second_expand: float32 [1152, 4, 1152], P('row', None, 'col'), may hold values from 1.47456 to 11.79648
- second_contract: float32 [4, 1152, 1152], P(None, 'col', 'row'), may hold values from 1.47456 to 11.79648
- second_bias_rows: float32 [8, 1152], P(None, 'row'), may hold values from 1.47456 to 11.79648
- second_bias_cols: float32 [6, 1152], P(None, 'col'), may hold values from 1.47456 to 11.79648
Outputs:
- layer_out: float32 [8192, 1152], P(('dp', 'col'), 'row')
- latents_grad: float32 [8192, 1152], P(('dp', 'col'), 'row')
- conditioning_grad: float32 [32, 1152], P('dp', 'col')
- new_modulation: float32 [1152, 6, 1152], P('col', None, 'row')
- new_attention_in: float32 [3, 1152, 1152], P(None, 'row', 'col')
- new_attention_out: float32 [1152, 1152], P('col', 'row')
- new_expand: float32 [1152, 4, 1152], P('row', None, 'col')
- new_contract: float32 [4, 1152, 1152], P(None, 'col', 'row')
- new_bias_rows: float32 [8, 1152], P(None, 'row')
- new_bias_cols: float32 [6, 1152], P(None, 'col')
- new_first_modulation: float32 [1152, 6, 1152], P('col', None, 'row')
- new_first_attention_in: float32 [3, 1152, 1152], P(None, 'row', 'col')
- new_first_attention_out: float32 [1152, 1152], P('col', 'row')
- new_first_expand: float32 [1152, 4, 1152], P('row', None, 'col')
- new_first_contract: float32 [4, 1152, 1152], P(None, 'col', 'row')
- new_first_bias_rows: float32 [8, 1152], P(None, 'row')
- new_first_bias_cols: float32 [6, 1152], P(None, 'col')
- new_second_modulation: float32 [1152, 6, 1152], P('col', None, 'row')
- new_second_attention_in: float32 [3, 1152, 1152], P(None, 'row', 'col')
- new_second_attention_out: float32 [1152, 1152], P('col', 'row')
- new_second_expand: float32 [1152, 4, 1152], P('row', None, 'col')
- new_second_contract: float32 [4, 1152, 1152], P(None, 'col', 'row')
- new_second_bias_rows: float32 [8, 1152], P(None, 'row')
- new_second_bias_cols: float32 [6, 1152], P(None, 'col')
The draws below stay inside these ranges and needn't reach their ends.
Inputs may be any that keep to these rules, and one draw needn't show every extreme that they name: `latents_in`: independent entries of mean zero and standard deviation 1. `conditioning`: independent entries of mean zero and standard deviation 1. `cotangent`: independent entries of mean zero and standard deviation 1. `modulation_weight`: independent entries of mean zero and standard deviation 1 / sqrt(1152). `attention_in`: independent entries of mean zero and standard deviation 1 / sqrt(1152). `attention_out`: independent entries of mean zero and standard deviation 4 / sqrt(1152). `expand_weight`: independent entries of mean zero and standard deviation 1 / sqrt(1152). `contract_weight`: independent entries of mean zero and standard deviation 1 / sqrt(4608). `bias_rows`: independent entries of mean zero and standard deviation 0.3. `bias_cols`: independent entries of mean zero and standard deviation 0.3. `first_modulation`: independent entries of mean zero and standard deviation 0.067 * sqrt(8192). `first_attention_in`: independent entries of mean zero and standard deviation 0.067 * sqrt(8192). `first_attention_out`: independent entries of mean zero and standard deviation 0.067 * sqrt(8192). `first_expand`: independent entries of mean zero and standard deviation 0.067 * sqrt(8192). `first_contract`: independent entries of mean zero and standard deviation 0.067 * sqrt(8192). `first_bias_rows`: independent entries of mean zero and standard deviation 0.067 * sqrt(8192). `first_bias_cols`: independent entries of mean zero and standard deviation 0.067 * sqrt(8192).
All inputs are finite; a program needn't handle non-finite values.
Results may differ from the reference program's by a relative error of at most 0.012.
The reference program's roundings to bfloat16 on the way count: a program that leaves them out, or rounds other values in their place, can miss the bound.
Values may be sent and summed in bfloat16 or wider, within the bound.
No kernel may reach another device: no remote copies, remote signals or barrier semaphores. Data moves between devices by JAX's collectives and lax.ppermute only.
A program may use at most 256 MiB of HBM per device.

```python
import math
import jax
import jax.numpy as jnp
from jax import lax

D = 1152
H = 16
HD = 72
FF = 4608
SEQ = 256
STEP = 10
LATENTS = 32
TOKENS = 8192


def normal_part(key, shape, scale):
    return jnp.clip(jax.random.normal(key, shape, jnp.float32), -4.0, 4.0) * scale


def draw_latents_in(key, part):
    key = jax.random.fold_in(key, 101)
    return normal_part(key, (TOKENS, D), 1.0)


def draw_conditioning(key, part):
    key = jax.random.fold_in(key, 102)
    return normal_part(key, (LATENTS, D), 1.0)


def draw_cotangent(key, part):
    key = jax.random.fold_in(key, 103)
    return normal_part(key, (TOKENS, D), 1.0)


def draw_modulation_weight(key, part):
    key = jax.random.fold_in(key, 104)
    return normal_part(key, (D, 6, D), D ** (-0.5))


def draw_attention_in(key, part):
    key = jax.random.fold_in(key, 105)
    return normal_part(key, (3, D, D), D ** (-0.5))


def draw_attention_out(key, part):
    key = jax.random.fold_in(key, 106)
    return normal_part(key, (D, D), 4.0 * D ** (-0.5))


def draw_expand_weight(key, part):
    key = jax.random.fold_in(key, 107)
    return normal_part(key, (D, 4, D), D ** (-0.5))


def draw_contract_weight(key, part):
    key = jax.random.fold_in(key, 108)
    return normal_part(key, (4, D, D), FF ** (-0.5))


def draw_bias_rows(key, part):
    key = jax.random.fold_in(key, 109)
    return normal_part(key, (8, D), 0.3)


def draw_bias_cols(key, part):
    key = jax.random.fold_in(key, 110)
    return normal_part(key, (6, D), 0.3)


def draw_first_modulation(key, part):
    key = jax.random.fold_in(key, 111)
    return normal_part(key, (D, 6, D), 0.067 * TOKENS ** 0.5)


def draw_first_attention_in(key, part):
    key = jax.random.fold_in(key, 112)
    return normal_part(key, (3, D, D), 0.067 * TOKENS ** 0.5)


def draw_first_attention_out(key, part):
    key = jax.random.fold_in(key, 113)
    return normal_part(key, (D, D), 0.067 * TOKENS ** 0.5)


def draw_first_expand(key, part):
    key = jax.random.fold_in(key, 114)
    return normal_part(key, (D, 4, D), 0.067 * TOKENS ** 0.5)


def draw_first_contract(key, part):
    key = jax.random.fold_in(key, 115)
    return normal_part(key, (4, D, D), 0.067 * TOKENS ** 0.5)


def draw_first_bias_rows(key, part):
    key = jax.random.fold_in(key, 116)
    return normal_part(key, (8, D), 0.067 * TOKENS ** 0.5)


def draw_first_bias_cols(key, part):
    key = jax.random.fold_in(key, 117)
    return normal_part(key, (6, D), 0.067 * TOKENS ** 0.5)


def steps_of(rng, dims, split, low, top_value):
    level = 1.0
    for position, shards_of in split:
        steps = jax.random.uniform(jax.random.fold_in(jax.random.fold_in(rng, 6), position), (shards_of,), jnp.float32, low / len(split), top_value / len(split))
        level = level * jnp.repeat(jnp.exp(steps), dims[position] // shards_of).reshape((-1,) + (1,) * (len(dims) - 1 - position))
    return level


def setup_inputs(seed: int = 0) -> dict:
    seeds = jax.random.split(jax.random.key(seed), 25)
    latents_in = draw_latents_in(jax.random.fold_in(seeds[24], 71), 0)
    conditioning = draw_conditioning(jax.random.fold_in(seeds[24], 71), 0)
    cotangent = draw_cotangent(jax.random.fold_in(seeds[24], 71), 0)
    modulation_weight = draw_modulation_weight(jax.random.fold_in(seeds[24], 71), 0)
    attention_in = draw_attention_in(jax.random.fold_in(seeds[24], 71), 0)
    attention_out = draw_attention_out(jax.random.fold_in(seeds[24], 71), 0)
    expand_weight = draw_expand_weight(jax.random.fold_in(seeds[24], 71), 0)
    contract_weight = draw_contract_weight(jax.random.fold_in(seeds[24], 71), 0)
    bias_rows = draw_bias_rows(jax.random.fold_in(seeds[24], 71), 0)
    bias_cols = draw_bias_cols(jax.random.fold_in(seeds[24], 71), 0)
    first_modulation = draw_first_modulation(jax.random.fold_in(seeds[24], 71), 0)
    first_attention_in = draw_first_attention_in(jax.random.fold_in(seeds[24], 71), 0)
    first_attention_out = draw_first_attention_out(jax.random.fold_in(seeds[24], 71), 0)
    first_expand = draw_first_expand(jax.random.fold_in(seeds[24], 71), 0)
    first_contract = draw_first_contract(jax.random.fold_in(seeds[24], 71), 0)
    first_bias_rows = draw_first_bias_rows(jax.random.fold_in(seeds[24], 71), 0)
    first_bias_cols = draw_first_bias_cols(jax.random.fold_in(seeds[24], 71), 0)
    second_modulation = jnp.clip(jnp.exp(math.log(11.79648) - 2.0794415 * jax.random.uniform(seeds[17], (D, 6, D), jnp.float32) ** steps_of(seeds[17], (D, 6, D), ((0, 2), (2, 4)), -0.2, 0.2)), 1.47456, 11.79648)
    second_attention_in = jnp.clip(jnp.exp(math.log(11.79648) - 2.0794415 * jax.random.uniform(seeds[18], (3, D, D), jnp.float32) ** steps_of(seeds[18], (3, D, D), ((1, 4), (2, 2)), -0.2, 0.2)), 1.47456, 11.79648)
    second_attention_out = jnp.clip(jnp.exp(math.log(11.79648) - 2.0794415 * jax.random.uniform(seeds[19], (D, D), jnp.float32) ** steps_of(seeds[19], (D, D), ((0, 2), (1, 4)), -0.2, 0.2)), 1.47456, 11.79648)
    second_expand = jnp.clip(jnp.exp(math.log(11.79648) - 2.0794415 * jax.random.uniform(seeds[20], (D, 4, D), jnp.float32) ** steps_of(seeds[20], (D, 4, D), ((0, 4), (2, 2)), -0.2, 0.2)), 1.47456, 11.79648)
    second_contract = jnp.clip(jnp.exp(math.log(11.79648) - 2.0794415 * jax.random.uniform(seeds[21], (4, D, D), jnp.float32) ** steps_of(seeds[21], (4, D, D), ((1, 2), (2, 4)), -0.2, 0.2)), 1.47456, 11.79648)
    second_bias_rows = jnp.clip(jnp.exp(math.log(11.79648) - 2.0794415 * jax.random.uniform(seeds[22], (8, D), jnp.float32) ** steps_of(seeds[22], (8, D), ((1, 4),), -0.2, 0.2)), 1.47456, 11.79648)
    second_bias_cols = jnp.clip(jnp.exp(math.log(11.79648) - 2.0794415 * jax.random.uniform(seeds[23], (6, D), jnp.float32) ** steps_of(seeds[23], (6, D), ((1, 2),), -0.2, 0.2)), 1.47456, 11.79648)
    return dict(latents_in=latents_in, conditioning=conditioning, cotangent=cotangent, modulation_weight=modulation_weight, attention_in=attention_in, attention_out=attention_out, expand_weight=expand_weight, contract_weight=contract_weight, bias_rows=bias_rows, bias_cols=bias_cols, first_modulation=first_modulation, first_attention_in=first_attention_in, first_attention_out=first_attention_out, first_expand=first_expand, first_contract=first_contract, first_bias_rows=first_bias_rows, first_bias_cols=first_bias_cols, second_modulation=second_modulation, second_attention_in=second_attention_in, second_attention_out=second_attention_out, second_expand=second_expand, second_contract=second_contract, second_bias_rows=second_bias_rows, second_bias_cols=second_bias_cols)


highest = lax.Precision.HIGHEST
norm_eps = 1e-06
beta_first = 0.9
beta_second = 0.999
adam_eps = 1e-08
weight_decay = 0.01

@jax.custom_vjp
def low(v):
    return lax.optimization_barrier(v.astype(jnp.bfloat16)).astype(jnp.float32)

@jax.custom_vjp
def low_back(v):
    return v

def low_keep(v):
    return (low(v), None)

def low_pass(kept, grad):
    return (grad,)

def back_keep(v):
    return (v, None)

def back_low(kept, grad):
    return (low(grad),)
low.defvjp(low_keep, low_pass)
low_back.defvjp(back_keep, back_low)

def layer_norm(stream):
    center = lax.optimization_barrier(jnp.mean(stream, -1, keepdims=True))
    spread = lax.optimization_barrier(jnp.mean(stream * stream, -1, keepdims=True)) - center * center
    return (stream - center) * lax.rsqrt(spread + norm_eps)

def forward(params, stream, condition):
    modulation_weight, attention_in, attention_out, expand_weight, contract_weight, bias_rows, bias_cols = params
    group_size = stream.shape[0]
    score_scale = 1.0 / math.sqrt(HD)
    silu_cond = low(jax.nn.silu(condition))
    modulation = low_back(jnp.einsum('gc,ckd->gkd', silu_cond, low(modulation_weight), precision=highest) + bias_rows[:6])
    members = [modulation[:, member][:, None, :] for member in range(6)]
    shift_one, scale_one, gate_one, shift_two, scale_two, gate_two = members
    act_one = low(layer_norm(stream) * (1.0 + scale_one) + shift_one)
    attend_low = low(attention_in)
    queries = low(low_back(jnp.einsum('gtd,de->gte', act_one, attend_low[0], precision=highest) + bias_cols[0]))
    key_rows = low(low_back(jnp.einsum('gtd,de->gte', act_one, attend_low[1], precision=highest)))
    values = low(low_back(jnp.einsum('gtd,de->gte', act_one, attend_low[2], precision=highest) + bias_cols[1]))
    shaped = (group_size, SEQ, H, HD)
    scores = low_back(jnp.einsum('gqhe,gkhe->ghqk', queries.reshape(shaped), key_rows.reshape(shaped), precision=highest) * score_scale)
    soft_weights = low(jax.nn.softmax(scores, axis=-1))
    attended = jnp.einsum('ghqk,gkhe->gqhe', soft_weights, values.reshape(shaped), precision=highest).reshape(group_size, SEQ, D)
    attended = low(low_back(attended))
    branch_one = low_back(jnp.einsum('gtd,de->gte', attended, low(attention_out), precision=highest) + bias_rows[6])
    middle = stream + gate_one * branch_one
    act_two = low(layer_norm(middle) * (1.0 + scale_two) + shift_two)
    hidden_pre = low_back(jnp.einsum('gtd,dkf->gtkf', act_two, low(expand_weight), precision=highest) + bias_cols[2:6])
    hidden = low(jax.nn.gelu(hidden_pre, approximate=True))
    branch_two = low_back(jnp.einsum('gtkf,kfd->gtd', hidden, low(contract_weight), precision=highest) + bias_rows[7])
    return middle + gate_two * branch_two

def rates_table():
    base_rate = 1.5 / math.sqrt(D)
    return (base_rate, base_rate, 4.0 * base_rate, base_rate, 1.5 / math.sqrt(FF), 0.45, 0.45)

def adamw(weight, first_old, second, gradient, learn_rate):
    first_new = beta_first * first_old + (1.0 - beta_first) * gradient
    second_new = beta_second * second + (1.0 - beta_second) * gradient * gradient
    first_hat = first_new / (1.0 - beta_first ** STEP)
    second_hat = second_new / (1.0 - beta_second ** STEP)
    weight_new = weight - learn_rate * (first_hat / (jnp.sqrt(second_hat) + adam_eps) + weight_decay * weight)
    return (weight_new, first_new, second_new)

def reference(latents_in, conditioning, cotangent, modulation_weight, attention_in, attention_out, expand_weight, contract_weight, bias_rows, bias_cols, first_modulation, first_attention_in, first_attention_out, first_expand, first_contract, first_bias_rows, first_bias_cols, second_modulation, second_attention_in, second_attention_out, second_expand, second_contract, second_bias_rows, second_bias_cols):
    params = (modulation_weight, attention_in, attention_out, expand_weight, contract_weight, bias_rows, bias_cols)
    firsts = (first_modulation, first_attention_in, first_attention_out, first_expand, first_contract, first_bias_rows, first_bias_cols)
    seconds = (second_modulation, second_attention_in, second_attention_out, second_expand, second_contract, second_bias_rows, second_bias_cols)
    group_size = math.gcd(LATENTS, 16)
    blocks = LATENTS // group_size
    streams = latents_in.reshape(blocks, group_size, SEQ, D)
    conditions = conditioning.reshape(blocks, group_size, D)
    cotangents = cotangent.reshape(blocks, group_size, SEQ, D)

    def scan_step(totals, sample):
        stream, condition, cotangent_block = sample
        output, pullback = jax.vjp(forward, params, stream, condition)
        grad_params, grad_stream, grad_condition = pullback(cotangent_block)
        totals = jax.tree.map(jnp.add, totals, grad_params)
        return (totals, (output, grad_stream, grad_condition))
    zero_tree = jax.tree.map(jnp.zeros_like, params)
    gradients, (outputs, grad_streams, grad_conditions) = lax.scan(scan_step, zero_tree, (streams, conditions, cotangents))
    rates = rates_table()
    states = [adamw(params[member], firsts[member], seconds[member], gradients[member], rates[member]) for member in range(7)]
    return (outputs.reshape(TOKENS, D), grad_streams.reshape(TOKENS, D), grad_conditions.reshape(LATENTS, D), states[0][0], states[1][0], states[2][0], states[3][0], states[4][0], states[5][0], states[6][0], states[0][1], states[1][1], states[2][1], states[3][1], states[4][1], states[5][1], states[6][1], states[0][2], states[1][2], states[2][2], states[3][2], states[4][2], states[5][2], states[6][2])
```

```python
import math

import jax
import jax.numpy as jnp
from jax import lax
from jax.sharding import PartitionSpec as P

D = 1152
HD = 72
FF = 4608
SEQ = 256
STEP = 10


norm_eps = 1e-06
beta_first = 0.9
beta_second = 0.999
adam_eps = 1e-08
weight_decay = 0.01

low_type = jnp.bfloat16
wide_type = jnp.float32


def rates_table():
    base_rate = 1.5 / math.sqrt(D)
    return (base_rate, base_rate, 4.0 * base_rate, base_rate, 1.5 / math.sqrt(FF), 0.45, 0.45)


def adamw(weight, first_old, second, gradient, learn_rate):
    first_new = beta_first * first_old + (1.0 - beta_first) * gradient
    second_new = beta_second * second + (1.0 - beta_second) * gradient * gradient
    first_hat = first_new / (1.0 - beta_first**STEP)
    second_hat = second_new / (1.0 - beta_second**STEP)
    weight_new = weight - learn_rate * (
        first_hat / (jnp.sqrt(second_hat) + adam_eps) + weight_decay * weight
    )
    return (weight_new, first_new, second_new)


def matmul(left_side, right_side):
    return jnp.dot(left_side, right_side, preferred_element_type=wide_type)


def matmul_nt(left_side, right_side):
    return lax.dot_general(
        left_side, right_side, (((1,), (1,)), ((), ())), preferred_element_type=wide_type
    )


def matmul_tn(left_side, right_side):
    return lax.dot_general(
        left_side, right_side, (((0,), (0,)), ((), ())), preferred_element_type=wide_type
    )


def swap(tensor, axis, size, bit):
    return lax.ppermute(tensor, axis, [(place, place ^ bit) for place in range(size)])


def row_swap(tensor, bit):
    return swap(tensor, "row", 4, bit)


def after(tensor, *others):
    return lax.optimization_barrier((tensor,) + others)[0]


def meet(*tensors):
    return lax.optimization_barrier(tensors)


def gather_cores(shard, came):
    chips = jnp.concatenate([shard, came], 0)
    return jnp.concatenate([chips, row_swap(chips, 1)], 0)


def width_halves(left_side, right_side):
    half = left_side.shape[1] // 2
    sent = matmul_tn(left_side[:, half:], right_side).astype(low_type)
    return (matmul_tn(left_side[:, :half], right_side), sent)


def latent_parts(blocks, chip):
    pairs = blocks.reshape((2, 2) + blocks.shape[1:])
    kept = lax.dynamic_index_in_dim(pairs, chip, 0, False)
    return (kept, lax.dynamic_index_in_dim(pairs, 1 - chip, 0, False))


def latent_cores(chips, core):
    both = jnp.stack(chips)
    kept = lax.dynamic_index_in_dim(both, core, 1, False)
    came = row_swap(lax.dynamic_index_in_dim(both, 1 - core, 1, False), 1)
    return jnp.concatenate([kept[0], kept[1], came[0], came[1]], -1)


def from_latent(whole, chip, core):
    width = whole.shape[-1] // 4
    parts = [whole[:, place * width : (place + 1) * width] for place in range(4)]
    other = row_swap(jnp.stack(parts[2:]), 1)
    mine = jnp.stack([parts[0], other[0]])
    far = row_swap(jnp.stack([parts[1], other[1]]), 2)
    pairs = jnp.stack([mine, far])
    pairs = jnp.where(core == 1, pairs[:, ::-1], pairs)
    pairs = jnp.where(chip == 1, pairs[::-1], pairs)
    return pairs.reshape((4,) + pairs.shape[2:])


def gather_axis(tensor, axis, size):
    bit = 1
    while bit < size:
        tensor = jnp.concatenate([tensor, swap(tensor, axis, size, bit)], 0)
        bit *= 2
    return tensor


def gather_groups(tensor, size):
    return jnp.concatenate(
        [tensor] + [swap(tensor, "dp", size, place) for place in range(1, size)], 0
    )


def scatter_axis(partial, axis, size):
    bit = size // 2
    while bit:
        half = partial.shape[0] // 2
        came = swap(partial[half:].astype(low_type), axis, size, bit)
        partial = partial[:half] + came.astype(wide_type)
        bit //= 2
    return partial


def sum_axis(tensor, axis, size):
    bit = 1
    while bit < size:
        tensor = tensor + swap(tensor, axis, size, bit)
        bit *= 2
    return tensor


def chips_parts(partial):
    half = partial.shape[0] // 2
    return (partial[:half], partial[half:].astype(low_type))


def groups_first(sent, size):
    if size != 4:
        return sent
    came = lax.ppermute(sent, "dp", [(0, 1), (3, 2)])
    return (sent.astype(wide_type) + came.astype(wide_type)).astype(low_type)


def groups_second(pair, size):
    if size != 4:
        return lax.psum(pair, "dp")
    came = lax.ppermute(pair, "dp", [(1, 2), (2, 1)])
    return (pair.astype(wide_type) + came.astype(wide_type)).astype(low_type)


def groups_third(total, size):
    if size != 4:
        return total
    place = lax.axis_index("dp")
    came = lax.ppermute(total, "dp", [(1, 0), (2, 3)])
    return jnp.where((place == 1) | (place == 2), total, came)


def normalize(stream):
    center = jnp.mean(stream, -1, keepdims=True)
    spread = jnp.mean(stream * stream, -1, keepdims=True) - center * center
    inverse = lax.rsqrt(spread + norm_eps)
    return ((stream - center) * inverse, inverse)


def normalize_back(grad_normed, normed, inverse):
    mean = jnp.mean(grad_normed, -1, keepdims=True)
    cross = jnp.mean(grad_normed * normed, -1, keepdims=True)
    return inverse * (grad_normed - mean - normed * cross)


def attention_forward(queries, key_rows, values):
    token_count, width = queries.shape
    shaped = (token_count // SEQ, SEQ, width // HD, HD)
    score_scale = 1.0 / math.sqrt(HD)
    scores = (
        jnp.einsum(
            "lqhe,lkhe->lhqk",
            queries.reshape(shaped),
            key_rows.reshape(shaped),
            preferred_element_type=wide_type,
        )
        * score_scale
    )
    row_max = jnp.max(scores, -1, keepdims=True)
    exponent = jnp.exp(scores - row_max)
    totals = jnp.sum(exponent, -1, keepdims=True)
    soft_weights = (exponent / totals).astype(low_type)
    attended = jnp.einsum(
        "lhqk,lkhe->lqhe", soft_weights, values.reshape(shaped), preferred_element_type=wide_type
    )
    return (attended.reshape(token_count, width).astype(low_type), row_max + jnp.log(totals))


def attention_backward(queries, key_rows, values, log_total, grad_attended):
    token_count, width = queries.shape
    shaped = (token_count // SEQ, SEQ, width // HD, HD)
    score_scale = 1.0 / math.sqrt(HD)
    query_heads = queries.reshape(shaped)
    key_heads = key_rows.reshape(shaped)
    value_heads = values.reshape(shaped)
    grad_heads = grad_attended.reshape(shaped)
    scores = (
        jnp.einsum("lqhe,lkhe->lhqk", query_heads, key_heads, preferred_element_type=wide_type)
        * score_scale
    )
    soft_float = jnp.exp(scores - log_total)
    grad_soft = jnp.einsum(
        "lqhe,lkhe->lhqk", grad_heads, value_heads, preferred_element_type=wide_type
    )
    grad_values = jnp.einsum(
        "lhqk,lqhe->lkhe",
        soft_float.astype(low_type),
        grad_heads,
        preferred_element_type=wide_type,
    )
    inner = jnp.sum(soft_float * grad_soft, -1, keepdims=True)
    grad_scores = (soft_float * (grad_soft - inner)).astype(low_type)
    grad_queries = (
        jnp.einsum("lhqk,lkhe->lqhe", grad_scores, key_heads, preferred_element_type=wide_type)
        * score_scale
    )
    grad_keys = (
        jnp.einsum("lhqk,lqhe->lkhe", grad_scores, query_heads, preferred_element_type=wide_type)
        * score_scale
    )
    joined = jnp.concatenate(
        [
            grad_queries.reshape(token_count, width),
            grad_keys.reshape(token_count, width),
            grad_values.reshape(token_count, width),
        ],
        1,
    )
    return joined.astype(low_type)


def on_device(
    group_count,
    col_count,
    latents_in,
    conditioning,
    cotangent,
    modulation_weight,
    attention_in,
    attention_out,
    expand_weight,
    contract_weight,
    bias_rows,
    bias_cols,
    first_modulation,
    first_attention_in,
    first_attention_out,
    first_expand,
    first_contract,
    first_bias_rows,
    first_bias_cols,
    second_modulation,
    second_attention_in,
    second_attention_out,
    second_expand,
    second_contract,
    second_bias_rows,
    second_bias_cols,
):
    width_row = latents_in.shape[1]
    width_col = attention_in.shape[2]
    row_place = lax.axis_index("row")
    chip, core = row_place // 2, row_place % 2
    col_place = lax.axis_index("col")

    stream_parts = latent_parts(latents_in.astype(low_type).reshape(4, SEQ, width_row), chip)
    conditioning_first = after(conditioning, stream_parts[1])
    silu_low = jax.nn.silu(conditioning_first).astype(low_type)
    modulation_low = modulation_weight.astype(low_type)
    modulation_part = jnp.einsum(
        "lc,ckr->lkr", silu_low, modulation_low, preferred_element_type=wide_type
    ).reshape(col_count, 4, 6, width_row)
    if col_count == 2:
        kept = lax.dynamic_index_in_dim(modulation_part, col_place, 0, False)
        sent = lax.dynamic_index_in_dim(modulation_part, 1 - col_place, 0, False)
        modulation_row = kept + swap(sent, "col", 2, 1)
    else:
        modulation_row = lax.psum_scatter(modulation_part, "col", scatter_dimension=0)
    modulation_row = jnp.concatenate(
        [modulation_row + bias_rows[:6], jnp.broadcast_to(bias_rows[6:], (4, 2, width_row))], 1
    )
    modulation_parts = latent_parts(modulation_row, chip)
    attend_shard = jnp.concatenate([attention_in[part].astype(low_type) for part in range(3)], 1)
    stream_came, modulation_came, attend_shard = meet(
        row_swap(stream_parts[1], 2), row_swap(modulation_parts[1], 2), attend_shard
    )
    modulation = latent_cores((modulation_parts[0], modulation_came), core)
    shift_one, scale_one, gate_one, shift_two, scale_two, gate_two, bias_out, bias_contract = [
        modulation[member : member + 1] for member in range(8)
    ]
    stream = latent_cores((stream_parts[0], stream_came), core).astype(wide_type)

    normed_one, inverse_one = normalize(stream)
    act_one = (normed_one * (1.0 + scale_one) + shift_one).astype(low_type)
    cotangent_late, output_late, expand_late, contract_late, act_one = meet(
        cotangent, attention_out, expand_weight, contract_weight, act_one
    )
    cotangent_parts = latent_parts(
        cotangent_late.astype(low_type).reshape(4, SEQ, width_row), chip
    )
    output_shard = output_late.astype(low_type).T
    expand_shard = expand_late.astype(low_type).reshape(width_row, 4 * width_col)
    contract_shard = contract_late.astype(low_type)
    contract_shard = contract_shard.reshape(4 * width_col, width_row).T
    act_one_all, attend_came, cotangent_sent, output_shard, expand_shard, contract_shard = meet(
        gather_axis(act_one, "col", col_count),
        row_swap(attend_shard, 2),
        cotangent_parts[1],
        output_shard,
        expand_shard,
        contract_shard,
    )
    attend_matrix = gather_cores(attend_shard, attend_came)
    attend_sums = matmul(act_one_all, attend_matrix)
    queries = (attend_sums[:, :width_col] + bias_cols[0]).astype(low_type)
    key_rows = attend_sums[:, width_col : 2 * width_col].astype(low_type)
    values = (attend_sums[:, 2 * width_col :] + bias_cols[1]).astype(low_type)
    queries, cotangent_came, output_came = meet(
        queries, row_swap(cotangent_sent, 2), row_swap(output_shard, 2)
    )
    stream_grad = latent_cores((cotangent_parts[0], cotangent_came), core).astype(wide_type)
    grad_branch_two = (gate_two * stream_grad).astype(low_type)
    attended, log_total = attention_forward(queries, key_rows, values)
    silu_order = jnp.stack(
        [
            lax.dynamic_index_in_dim(
                silu_low.reshape(col_count, 4, width_col), col_place ^ place, 0, False
            )
            for place in range(col_count)
        ]
    )
    silu_group = after(silu_order.reshape(4 * col_count, width_col), queries)
    output_matrix = gather_cores(output_shard, output_came)
    branch_one_part = matmul_nt(attended, output_matrix)
    branch_one_part, grad_branch_two_all, silu_all = meet(
        branch_one_part,
        gather_axis(grad_branch_two, "col", col_count),
        gather_groups(silu_group, group_count),
    )
    branch_one, expand_came, contract_came = meet(
        scatter_axis(branch_one_part, "col", col_count),
        row_swap(expand_shard, 2),
        row_swap(contract_shard[:, : 2 * width_col], 2),
    )
    branch_one = branch_one + bias_out
    expand_matrix = gather_cores(expand_shard, expand_came)
    step_one = gate_one * branch_one
    middle = stream + step_one
    normed_two, inverse_two = normalize(middle)
    act_two = (normed_two * (1.0 + scale_two) + shift_two).astype(low_type)
    act_two_all, expand_matrix, contract_late = meet(
        gather_axis(act_two, "col", col_count),
        expand_matrix,
        row_swap(contract_shard[:, 2 * width_col :], 2),
    )
    contract_matrix = gather_cores(
        contract_shard, jnp.concatenate([contract_came, contract_late], 1)
    )
    hidden_pre = matmul(act_two_all, expand_matrix) + bias_cols[2:6].reshape(-1)
    hidden, gelu_pull = jax.vjp(lambda value: jax.nn.gelu(value, approximate=True), hidden_pre)
    hidden = hidden.astype(low_type)

    grad_hidden_act = matmul(grad_branch_two_all, contract_matrix)
    grad_hidden = gelu_pull(grad_hidden_act)[0].astype(low_type)
    grad_act_two_part = matmul_nt(grad_hidden, expand_matrix)
    hidden, grad_act_two_part = meet(hidden, grad_act_two_part)
    contract_kept, contract_sent = width_halves(grad_branch_two_all, hidden)
    branch_two_part = matmul_nt(after(hidden, contract_sent), contract_matrix)
    grad_act_two, contract_kept, contract_came, branch_two_part = meet(
        scatter_axis(grad_act_two_part, "col", col_count),
        contract_kept,
        row_swap(contract_sent, 1),
        branch_two_part,
    )
    contract_parts = chips_parts(contract_kept + contract_came.astype(wide_type))
    grad_shift_two = jnp.sum(grad_act_two, 0)
    grad_scale_two = jnp.sum(grad_act_two * normed_two, 0)
    back_two = normalize_back(grad_act_two * (1.0 + scale_two), normed_two, inverse_two)
    grad_middle = stream_grad + back_two
    grad_gate_one = jnp.sum(grad_middle * branch_one, 0)

    grad_branch_one = (gate_one * grad_middle).astype(low_type)
    grad_branch_one, contract_sent = meet(grad_branch_one, contract_parts[1])
    expand_kept, expand_sent = width_halves(after(act_two_all, grad_branch_one), grad_hidden)
    grad_branch_one_all, expand_kept, expand_came = meet(
        gather_axis(grad_branch_one, "col", col_count),
        expand_kept,
        row_swap(expand_sent, 1),
    )
    grad_attended = matmul(grad_branch_one_all, output_matrix).astype(low_type)
    expand_parts = chips_parts(expand_kept + expand_came.astype(wide_type))
    grad_attended, expand_sent = meet(grad_attended, expand_parts[1])
    grad_attend = attention_backward(queries, key_rows, values, log_total, grad_attended)
    grad_attend, contract_came = meet(grad_attend, row_swap(contract_sent, 2))
    grad_act_one_part = matmul_nt(grad_attend, attend_matrix)
    contract_low = (contract_parts[0] + contract_came.astype(wide_type)).astype(low_type)
    grad_act_one_part, contract_low = meet(grad_act_one_part, contract_low)
    attend_all = after(grad_attend, grad_act_one_part)
    value_kept, value_sent = width_halves(act_one_all, attend_all[:, 2 * width_col :])
    output_kept, output_sent = width_halves(
        after(grad_branch_one_all, grad_act_one_part), attended
    )
    inner_kept, inner_sent = width_halves(act_one_all, attend_all[:, : 2 * width_col])
    outer_kept = jnp.concatenate([output_kept, value_kept, inner_kept], 1)
    outer_sent = jnp.concatenate([output_sent, value_sent, inner_sent], 1)
    grad_cols = jnp.concatenate(
        [
            jnp.sum(grad_hidden, 0, dtype=wide_type),
            jnp.sum(attend_all[:, :width_col], 0, dtype=wide_type),
            jnp.sum(attend_all[:, 2 * width_col :], 0, dtype=wide_type),
            jnp.zeros((2 * width_col,), wide_type),
        ]
    ).reshape(2, 4 * width_col)
    grad_act_one, branch_two, outer_kept, outer_came, expand_came, contract_first, cols_came = meet(
        scatter_axis(grad_act_one_part, "col", col_count),
        scatter_axis(branch_two_part, "col", col_count),
        outer_kept,
        row_swap(outer_sent, 1),
        row_swap(expand_sent, 2),
        groups_first(contract_low, group_count),
        row_swap(grad_cols, 1),
    )
    branch_two = branch_two + bias_contract
    outer_parts = chips_parts(outer_kept + outer_came.astype(wide_type))
    grad_cols = grad_cols + cols_came
    expand_low = (expand_parts[0] + expand_came.astype(wide_type)).astype(low_type)
    grad_act_one, expand_low, outer_sent, grad_cols = meet(
        grad_act_one, expand_low, outer_parts[1], grad_cols
    )
    grad_shift_one = jnp.sum(grad_act_one, 0)
    grad_scale_one = jnp.sum(grad_act_one * normed_one, 0)
    back_one = normalize_back(grad_act_one * (1.0 + scale_one), normed_one, inverse_one)
    grad_gate_two = jnp.sum(stream_grad * branch_two, 0)

    grad_own = jnp.stack(
        [
            grad_shift_one,
            grad_scale_one,
            grad_gate_one,
            grad_shift_two,
            grad_scale_two,
            grad_gate_two,
            jnp.sum(grad_branch_one, 0, dtype=wide_type),
            jnp.sum(grad_branch_two, 0, dtype=wide_type),
        ]
    ).astype(low_type)
    grad_row = from_latent(grad_own, chip, core)
    grad_group = gather_axis(grad_row[None], "col", col_count)
    grad_group, contract_second, expand_first, outer_came, cols_came = meet(
        grad_group.reshape(4 * col_count, 8, width_row),
        groups_second(contract_first, group_count),
        groups_first(expand_low, group_count),
        row_swap(outer_sent, 2),
        row_swap(grad_cols, 2),
    )
    outer_low = (outer_parts[0] + outer_came.astype(wide_type)).astype(low_type)
    cols_low = jnp.pad(grad_cols + cols_came, ((0, 14), (0, 0))).astype(low_type)
    outer_low = jnp.concatenate([outer_low, cols_low])
    grad_all, outer_low = meet(gather_groups(grad_group, group_count), outer_low)
    contract_second, expand_first, outer_low, grad_all = meet(
        contract_second, expand_first, outer_low, grad_all
    )
    grad_modulation_weight = jnp.einsum(
        "lc,lkr->ckr", silu_all, grad_all[:, :6], preferred_element_type=wide_type
    )
    rates = rates_table()
    state_modulation = adamw(
        modulation_weight, first_modulation, second_modulation, grad_modulation_weight, rates[0]
    )
    mark, contract_third, expand_second, outer_first = meet(
        state_modulation[0],
        groups_third(contract_second, group_count),
        groups_second(expand_first, group_count),
        groups_first(outer_low, group_count),
    )
    state_modulation = (mark,) + state_modulation[1:]
    grad_contract_weight = contract_third.T.reshape(4, width_col, width_row).astype(wide_type)
    state_contract = adamw(
        contract_weight, first_contract, second_contract, grad_contract_weight, rates[4]
    )
    shown_low = after((step_one + gate_two * branch_two).astype(low_type), contract_third)
    shown = from_latent(shown_low, chip, core)
    shown_grad_low = after((back_two + back_one).astype(low_type), contract_third)
    shown_grad = from_latent(shown_grad_low, chip, core)
    layer_out = latents_in + shown.astype(wide_type).reshape(latents_in.shape)
    latents_grad = cotangent + shown_grad.astype(wide_type).reshape(cotangent.shape)

    grad_rows = jnp.sum(grad_all, 0, dtype=wide_type)
    silu_part = jnp.einsum(
        "lkr,ckr->lc",
        after(grad_group[:, :6], contract_third),
        modulation_low,
        preferred_element_type=wide_type,
    )
    grad_silu_order = sum_axis(silu_part, "row", 4).reshape(col_count, 4, width_col)
    grad_silu = jnp.stack(
        [
            lax.dynamic_index_in_dim(grad_silu_order, col_place ^ place, 0, False)
            for place in range(col_count)
        ]
    ).reshape(4 * col_count, width_col)
    mark, layer_out, latents_grad, grad_silu, expand_third, outer_second = meet(
        state_contract[0],
        layer_out,
        latents_grad,
        grad_silu,
        groups_third(expand_second, group_count),
        groups_second(outer_first, group_count),
    )
    state_contract = (mark,) + state_contract[1:]
    grad_expand_weight = expand_third.reshape(width_row, 4, width_col).astype(wide_type)
    state_expand = adamw(
        expand_weight, first_expand, second_expand, grad_expand_weight, rates[3]
    )
    mark, attend_total = meet(state_expand[0], groups_third(outer_second, group_count))
    state_expand = (mark,) + state_expand[1:]
    silu_value, silu_pull = jax.vjp(jax.nn.silu, conditioning)
    conditioning_grad = silu_pull(grad_silu)[0]

    cols_total = attend_total[width_row : width_row + 2].reshape(-1)[: 6 * width_col]
    cols_total = cols_total.reshape(6, width_col).astype(wide_type)
    grad_cols = jnp.concatenate([cols_total[4:], cols_total[:4]])
    attend_total = attend_total[:width_row]
    grad_attend_weight = jnp.stack(
        [
            attend_total[:, 2 * width_col : 3 * width_col],
            attend_total[:, 3 * width_col :],
            attend_total[:, width_col : 2 * width_col],
        ]
    ).astype(wide_type)
    grad_output_weight = attend_total[:, :width_col].T.astype(wide_type)
    states = [
        state_modulation,
        adamw(
            attention_in, first_attention_in, second_attention_in, grad_attend_weight, rates[1]
        ),
        adamw(
            attention_out, first_attention_out, second_attention_out, grad_output_weight, rates[2]
        ),
        state_expand,
        state_contract,
        adamw(bias_rows, first_bias_rows, second_bias_rows, grad_rows, rates[5]),
        adamw(bias_cols, first_bias_cols, second_bias_cols, grad_cols, rates[6]),
    ]
    return tuple(
        [layer_out, latents_grad, conditioning_grad]
        + [states[member][0] for member in range(7)]
        + [states[member][1] for member in range(7)]
        + [states[member][2] for member in range(7)]
    )


def solution(mesh):
    token_spec = P(("dp", "col"), "row")
    state_specs = (
        P("col", None, "row"),
        P(None, "row", "col"),
        P("col", "row"),
        P("row", None, "col"),
        P(None, "col", "row"),
        P(None, "row"),
        P(None, "col"),
    )
    in_specs = (token_spec, P("dp", "col"), token_spec) + state_specs * 3
    out_specs = (token_spec, token_spec, P("dp", "col")) + state_specs * 3

    def body(*arrays):
        return on_device(mesh.shape["dp"], mesh.shape["col"], *arrays)

    return jax.shard_map(
        body, mesh=mesh, in_specs=in_specs, out_specs=out_specs, check_vma=False
    )
```

```python
import math

import jax
import jax.numpy as jnp
from jax import lax
from jax.sharding import PartitionSpec as P

D = 1152
HD = 72
FF = 4608
SEQ = 256
STEP = 10


norm_eps = 1e-06
beta_first = 0.9
beta_second = 0.999
adam_eps = 1e-08
weight_decay = 0.01

low_type = jnp.bfloat16
wide_type = jnp.float32


def rates_table():
    base_rate = 1.5 / math.sqrt(D)
    return (base_rate, base_rate, 4.0 * base_rate, base_rate, 1.5 / math.sqrt(FF), 0.45, 0.45)


def adamw(weight, first_old, second, gradient, learn_rate):
    first_new = beta_first * first_old + (1.0 - beta_first) * gradient
    second_new = beta_second * second + (1.0 - beta_second) * gradient * gradient
    first_hat = first_new / (1.0 - beta_first**STEP)
    second_hat = second_new / (1.0 - beta_second**STEP)
    weight_new = weight - learn_rate * (
        first_hat / (jnp.sqrt(second_hat) + adam_eps) + weight_decay * weight
    )
    return (weight_new, first_new, second_new)


def matmul(left_side, right_side):
    return jnp.dot(left_side, right_side, preferred_element_type=wide_type)


def matmul_nt(left_side, right_side):
    return lax.dot_general(
        left_side, right_side, (((1,), (1,)), ((), ())), preferred_element_type=wide_type
    )


def matmul_tn(left_side, right_side):
    return lax.dot_general(
        left_side, right_side, (((0,), (0,)), ((), ())), preferred_element_type=wide_type
    )


def swap(tensor, axis, size, bit):
    return lax.ppermute(tensor, axis, [(place, place ^ bit) for place in range(size)])


def row_swap(tensor, bit):
    return swap(tensor, "row", 4, bit)


def after(tensor, *others):
    return lax.optimization_barrier((tensor,) + others)[0]


def meet(*tensors):
    return lax.optimization_barrier(tensors)


def gather_cores(shard, came):
    chips = jnp.concatenate([shard, came], 0)
    return jnp.concatenate([chips, row_swap(chips, 1)], 0)


def width_halves(left_side, right_side):
    half = left_side.shape[1] // 2
    sent = matmul_tn(left_side[:, half:], right_side).astype(low_type)
    return (matmul_tn(left_side[:, :half], right_side), sent)


def latent_parts(blocks, chip):
    pairs = blocks.reshape((2, 2) + blocks.shape[1:])
    kept = lax.dynamic_index_in_dim(pairs, chip, 0, False)
    return (kept, lax.dynamic_index_in_dim(pairs, 1 - chip, 0, False))


def latent_cores(chips, core):
    both = jnp.stack(chips)
    kept = lax.dynamic_index_in_dim(both, core, 1, False)
    came = row_swap(lax.dynamic_index_in_dim(both, 1 - core, 1, False), 1)
    return jnp.concatenate([kept[0], kept[1], came[0], came[1]], -1)


def from_latent(whole, chip, core):
    width = whole.shape[-1] // 4
    parts = [whole[:, place * width : (place + 1) * width] for place in range(4)]
    other = row_swap(jnp.stack(parts[2:]), 1)
    mine = jnp.stack([parts[0], other[0]])
    far = row_swap(jnp.stack([parts[1], other[1]]), 2)
    pairs = jnp.stack([mine, far])
    pairs = jnp.where(core == 1, pairs[:, ::-1], pairs)
    pairs = jnp.where(chip == 1, pairs[::-1], pairs)
    return pairs.reshape((4,) + pairs.shape[2:])


def gather_axis(tensor, axis, size):
    bit = 1
    while bit < size:
        tensor = jnp.concatenate([tensor, swap(tensor, axis, size, bit)], 0)
        bit *= 2
    return tensor


def gather_groups(tensor, size):
    return jnp.concatenate(
        [tensor] + [swap(tensor, "dp", size, place) for place in range(1, size)], 0
    )


def scatter_product(multiply, left_side, size):
    half = left_side.shape[0] // 2
    if size == 2:
        sent = multiply(left_side[half:]).astype(low_type)
        return (multiply(left_side[:half]), swap(sent, "col", size, 1))
    partial = multiply(left_side)
    bit = size // 2
    while bit > 1:
        half = partial.shape[0] // 2
        came = swap(partial[half:].astype(low_type), "col", size, bit)
        partial = partial[:half] + came.astype(wide_type)
        bit //= 2
    half = partial.shape[0] // 2
    return (partial[:half], swap(partial[half:].astype(low_type), "col", size, 1))


def sum_axis(tensor, axis, size):
    bit = 1
    while bit < size:
        tensor = tensor + swap(tensor, axis, size, bit)
        bit *= 2
    return tensor


def chips_parts(partial):
    half = partial.shape[0] // 2
    return (partial[:half], partial[half:].astype(low_type))


def groups_first_came(sent, size):
    if size != 4:
        return jnp.zeros_like(sent)
    return lax.ppermute(sent, "dp", [(0, 1), (3, 2)])


def groups_second_came(pair, size):
    if size != 4:
        return (lax.psum(pair, "dp").astype(wide_type) - pair.astype(wide_type)).astype(low_type)
    return lax.ppermute(pair, "dp", [(1, 2), (2, 1)])


def groups_third_came(total, size):
    if size != 4:
        return total
    return lax.ppermute(total, "dp", [(1, 0), (2, 3)])


def groups_add(kept, came):
    return (kept.astype(wide_type) + came.astype(wide_type)).astype(low_type)


def groups_choose(total, came, size):
    place = lax.axis_index("dp")
    return jnp.where((place == 1) | (place == 2) | (size != 4), total, came)


def normalize(stream):
    center = jnp.mean(stream, -1, keepdims=True)
    spread = jnp.mean(stream * stream, -1, keepdims=True) - center * center
    inverse = lax.rsqrt(spread + norm_eps)
    return ((stream - center) * inverse, inverse)


def normalize_back(grad_normed, normed, inverse):
    mean = jnp.mean(grad_normed, -1, keepdims=True)
    cross = jnp.mean(grad_normed * normed, -1, keepdims=True)
    return inverse * (grad_normed - mean - normed * cross)


def attention_forward(queries, key_rows, values):
    token_count, width = queries.shape
    shaped = (token_count // SEQ, SEQ, width // HD, HD)
    score_scale = 1.0 / math.sqrt(HD)
    scores = (
        jnp.einsum(
            "lqhe,lkhe->lhqk",
            queries.reshape(shaped),
            key_rows.reshape(shaped),
            preferred_element_type=wide_type,
        )
        * score_scale
    )
    row_max = jnp.max(scores, -1, keepdims=True)
    exponent = jnp.exp(scores - row_max)
    totals = jnp.sum(exponent, -1, keepdims=True)
    soft_weights = (exponent / totals).astype(low_type)
    attended = jnp.einsum(
        "lhqk,lkhe->lqhe", soft_weights, values.reshape(shaped), preferred_element_type=wide_type
    )
    return (attended.reshape(token_count, width).astype(low_type), row_max + jnp.log(totals))


def attention_backward(queries, key_rows, values, log_total, grad_attended):
    token_count, width = queries.shape
    shaped = (token_count // SEQ, SEQ, width // HD, HD)
    score_scale = 1.0 / math.sqrt(HD)
    query_heads = queries.reshape(shaped)
    key_heads = key_rows.reshape(shaped)
    value_heads = values.reshape(shaped)
    grad_heads = grad_attended.reshape(shaped)
    scores = (
        jnp.einsum("lqhe,lkhe->lhqk", query_heads, key_heads, preferred_element_type=wide_type)
        * score_scale
    )
    soft_float = jnp.exp(scores - log_total)
    grad_soft = jnp.einsum(
        "lqhe,lkhe->lhqk", grad_heads, value_heads, preferred_element_type=wide_type
    )
    grad_values = jnp.einsum(
        "lhqk,lqhe->lkhe",
        soft_float.astype(low_type),
        grad_heads,
        preferred_element_type=wide_type,
    )
    inner = jnp.sum(soft_float * grad_soft, -1, keepdims=True)
    grad_scores = (soft_float * (grad_soft - inner)).astype(low_type)
    grad_queries = (
        jnp.einsum("lhqk,lkhe->lqhe", grad_scores, key_heads, preferred_element_type=wide_type)
        * score_scale
    )
    grad_keys = (
        jnp.einsum("lhqk,lqhe->lkhe", grad_scores, query_heads, preferred_element_type=wide_type)
        * score_scale
    )
    joined = jnp.concatenate(
        [
            grad_queries.reshape(token_count, width),
            grad_keys.reshape(token_count, width),
            grad_values.reshape(token_count, width),
        ],
        1,
    )
    return joined.astype(low_type)


def on_device(
    group_count,
    col_count,
    latents_in,
    conditioning,
    cotangent,
    modulation_weight,
    attention_in,
    attention_out,
    expand_weight,
    contract_weight,
    bias_rows,
    bias_cols,
    first_modulation,
    first_attention_in,
    first_attention_out,
    first_expand,
    first_contract,
    first_bias_rows,
    first_bias_cols,
    second_modulation,
    second_attention_in,
    second_attention_out,
    second_expand,
    second_contract,
    second_bias_rows,
    second_bias_cols,
):
    width_row = latents_in.shape[1]
    width_col = attention_in.shape[2]
    row_place = lax.axis_index("row")
    chip, core = row_place // 2, row_place % 2
    col_place = lax.axis_index("col")

    stream_parts = latent_parts(latents_in.astype(low_type).reshape(4, SEQ, width_row), chip)
    conditioning_first = after(conditioning, stream_parts[1])
    silu_low = jax.nn.silu(conditioning_first).astype(low_type)
    modulation_low = modulation_weight.astype(low_type)
    modulation_part = jnp.einsum(
        "lc,ckr->lkr", silu_low, modulation_low, preferred_element_type=wide_type
    ).reshape(col_count, 4, 6, width_row)
    if col_count == 2:
        kept = lax.dynamic_index_in_dim(modulation_part, col_place, 0, False)
        sent = lax.dynamic_index_in_dim(modulation_part, 1 - col_place, 0, False)
        modulation_row = kept + swap(sent, "col", 2, 1)
    else:
        modulation_row = lax.psum_scatter(modulation_part, "col", scatter_dimension=0)
    modulation_row = jnp.concatenate(
        [modulation_row + bias_rows[:6], jnp.broadcast_to(bias_rows[6:], (4, 2, width_row))], 1
    )
    modulation_parts = latent_parts(modulation_row, chip)
    attend_shard = jnp.concatenate([attention_in[part].astype(low_type) for part in range(3)], 1)
    stream_came, modulation_came, attend_shard = meet(
        row_swap(stream_parts[1], 2), row_swap(modulation_parts[1], 2), attend_shard
    )
    modulation = latent_cores((modulation_parts[0], modulation_came), core)
    shift_one, scale_one, gate_one, shift_two, scale_two, gate_two, bias_out, bias_contract = [
        modulation[member : member + 1] for member in range(8)
    ]
    stream = latent_cores((stream_parts[0], stream_came), core).astype(wide_type)

    normed_one, inverse_one = normalize(stream)
    act_one = (normed_one * (1.0 + scale_one) + shift_one).astype(low_type)
    cotangent_late, output_late, expand_late, contract_late, act_one = meet(
        cotangent, attention_out, expand_weight, contract_weight, act_one
    )
    cotangent_parts = latent_parts(
        cotangent_late.astype(low_type).reshape(4, SEQ, width_row), chip
    )
    output_shard = output_late.astype(low_type).T
    expand_shard = expand_late.astype(low_type).reshape(width_row, 4 * width_col)
    contract_shard = contract_late.astype(low_type)
    contract_shard = contract_shard.reshape(4 * width_col, width_row).T
    act_one_all, attend_came, cotangent_sent, output_shard, expand_shard, contract_shard = meet(
        gather_axis(act_one, "col", col_count),
        row_swap(attend_shard, 2),
        cotangent_parts[1],
        output_shard,
        expand_shard,
        contract_shard,
    )
    attend_matrix = gather_cores(attend_shard, attend_came)
    attend_sums = matmul(act_one_all, attend_matrix)
    queries = (attend_sums[:, :width_col] + bias_cols[0]).astype(low_type)
    key_rows = attend_sums[:, width_col : 2 * width_col].astype(low_type)
    values = (attend_sums[:, 2 * width_col :] + bias_cols[1]).astype(low_type)
    queries, contract_shard = meet(queries, contract_shard)
    attended, log_total = attention_forward(queries, key_rows, values)
    attended, output_came, cotangent_came = meet(
        attended, row_swap(output_shard, 2), row_swap(cotangent_sent, 2)
    )
    silu_order = jnp.stack(
        [
            lax.dynamic_index_in_dim(
                silu_low.reshape(col_count, 4, width_col), col_place ^ place, 0, False
            )
            for place in range(col_count)
        ]
    )
    output_matrix = gather_cores(output_shard, output_came)
    stream_grad = latent_cores((cotangent_parts[0], cotangent_came), core).astype(wide_type)
    grad_branch_two = (gate_two * stream_grad).astype(low_type)
    branch_one_own, branch_one_came = scatter_product(
        lambda left_side: matmul_nt(left_side, output_matrix), attended, col_count
    )
    branch_one_own, expand_came, grad_branch_two = meet(
        branch_one_own, row_swap(expand_shard, 2), grad_branch_two
    )
    expand_matrix = gather_cores(expand_shard, expand_came)
    branch_one_own, branch_one_came, contract_came, grad_branch_two_all = meet(
        branch_one_own,
        branch_one_came,
        row_swap(contract_shard, 2),
        gather_axis(grad_branch_two, "col", col_count),
    )
    branch_one = branch_one_own + branch_one_came.astype(wide_type) + bias_out
    step_one = gate_one * branch_one
    middle = stream + step_one
    normed_two, inverse_two = normalize(middle)
    act_two = (normed_two * (1.0 + scale_two) + shift_two).astype(low_type)
    contract_matrix = gather_cores(contract_shard, contract_came)
    silu_group = after(silu_order.reshape(4 * col_count, width_col), act_two)
    act_two_all, expand_matrix, silu_all = meet(
        gather_axis(act_two, "col", col_count),
        expand_matrix,
        gather_groups(silu_group, group_count),
    )
    hidden_pre = matmul(act_two_all, expand_matrix) + bias_cols[2:6].reshape(-1)
    hidden, gelu_pull = jax.vjp(lambda value: jax.nn.gelu(value, approximate=True), hidden_pre)
    hidden = hidden.astype(low_type)

    grad_hidden_act = matmul(grad_branch_two_all, contract_matrix)
    grad_hidden = gelu_pull(grad_hidden_act)[0].astype(low_type)
    grad_act_two_own, grad_act_two_came = scatter_product(
        lambda left_side: matmul_nt(left_side, expand_matrix), grad_hidden, col_count
    )
    hidden, grad_act_two_own = meet(hidden, grad_act_two_own)
    contract_kept, contract_sent = width_halves(grad_branch_two_all, hidden)
    branch_two_own, branch_two_came = scatter_product(
        lambda left_side: matmul_nt(left_side, contract_matrix),
        after(hidden, contract_sent),
        col_count,
    )
    grad_act_two_own, grad_act_two_came, contract_kept, contract_came, branch_two_own = meet(
        grad_act_two_own,
        grad_act_two_came,
        contract_kept,
        row_swap(contract_sent, 1),
        branch_two_own,
    )
    grad_act_two = grad_act_two_own + grad_act_two_came.astype(wide_type)
    contract_parts = chips_parts(contract_kept + contract_came.astype(wide_type))
    grad_act_two, contract_sent = meet(grad_act_two, contract_parts[1])
    grad_shift_two = jnp.sum(grad_act_two, 0)
    grad_scale_two = jnp.sum(grad_act_two * normed_two, 0)
    back_two = normalize_back(grad_act_two * (1.0 + scale_two), normed_two, inverse_two)
    grad_middle = stream_grad + back_two
    grad_gate_one = jnp.sum(grad_middle * branch_one, 0)

    grad_branch_one = (gate_one * grad_middle).astype(low_type)
    expand_kept, expand_sent = width_halves(after(act_two_all, grad_branch_one), grad_hidden)
    grad_branch_one_all, expand_kept, expand_came = meet(
        gather_axis(grad_branch_one, "col", col_count),
        expand_kept,
        row_swap(expand_sent, 1),
    )
    grad_attended = matmul(grad_branch_one_all, output_matrix).astype(low_type)
    expand_parts = chips_parts(expand_kept + expand_came.astype(wide_type))
    grad_attended, expand_sent = meet(grad_attended, expand_parts[1])
    grad_attend = attention_backward(queries, key_rows, values, log_total, grad_attended)
    grad_attend, contract_came = meet(grad_attend, row_swap(contract_sent, 2))
    contract_low = (contract_parts[0] + contract_came.astype(wide_type)).astype(low_type)
    grad_attend, contract_low = meet(grad_attend, contract_low)
    grad_act_one_own, grad_act_one_came = scatter_product(
        lambda left_side: matmul_nt(left_side, attend_matrix), grad_attend, col_count
    )
    attend_all, grad_branch_one_all, grad_act_one_own = meet(
        grad_attend, grad_branch_one_all, grad_act_one_own
    )
    halves = [
        width_halves(act_one_all, attend_all[:, : 2 * width_col]),
        width_halves(grad_branch_one_all, attended),
        width_halves(act_one_all, attend_all[:, 2 * width_col :]),
    ]
    grad_cols = jnp.concatenate(
        [
            jnp.sum(grad_hidden, 0, dtype=wide_type),
            jnp.sum(attend_all[:, :width_col], 0, dtype=wide_type),
            jnp.sum(attend_all[:, 2 * width_col :], 0, dtype=wide_type),
            jnp.zeros((2 * width_col,), wide_type),
        ]
    ).reshape(2, 4 * width_col)
    grad_act_one_own, grad_act_one_came, branch_two_came, expand_came, contract_first, *pieces = meet(
        grad_act_one_own,
        grad_act_one_came,
        branch_two_came,
        row_swap(expand_sent, 2),
        groups_first_came(contract_low, group_count),
        *[kept for kept, _ in halves],
        *[row_swap(sent, 1) for _, sent in halves],
    )
    attend_parts = [
        chips_parts(kept + came.astype(wide_type)) for kept, came in zip(pieces[:3], pieces[3:])
    ]
    attend_sent = jnp.concatenate([sent for _, sent in attend_parts], 1)
    expand_low = (expand_parts[0] + expand_came.astype(wide_type)).astype(low_type)
    contract_pair = groups_add(contract_low, contract_first)
    contract_pair, expand_low, attend_sent, grad_act_one_own = meet(
        contract_pair, expand_low, attend_sent, grad_act_one_own
    )
    branch_two = branch_two_own + branch_two_came.astype(wide_type) + bias_contract
    grad_gate_two = jnp.sum(stream_grad * branch_two, 0)
    grad_act_one = grad_act_one_own + grad_act_one_came.astype(wide_type)
    grad_shift_one = jnp.sum(grad_act_one, 0)
    grad_scale_one = jnp.sum(grad_act_one * normed_one, 0)
    back_one = normalize_back(grad_act_one * (1.0 + scale_one), normed_one, inverse_one)

    grad_own = jnp.stack(
        [
            grad_shift_one,
            grad_scale_one,
            grad_gate_one,
            grad_shift_two,
            grad_scale_two,
            grad_gate_two,
            jnp.sum(grad_branch_one, 0, dtype=wide_type),
            jnp.sum(grad_branch_two, 0, dtype=wide_type),
        ]
    ).astype(low_type)
    grad_row = from_latent(grad_own, chip, core)
    grad_group = gather_axis(grad_row[None], "col", col_count)
    grad_cols = grad_cols + row_swap(after(grad_cols, grad_own), 1)
    grad_group, contract_came, expand_first, attend_came, cols_came = meet(
        grad_group.reshape(4 * col_count, 8, width_row),
        groups_second_came(contract_pair, group_count),
        groups_first_came(expand_low, group_count),
        row_swap(attend_sent, 2),
        row_swap(grad_cols, 2),
    )
    contract_total = groups_add(contract_pair, contract_came)
    expand_pair = groups_add(expand_low, expand_first)
    attend_low = jnp.concatenate([kept for kept, _ in attend_parts], 1)
    attend_low = (attend_low + attend_came.astype(wide_type)).astype(low_type)
    cols_low = jnp.pad(grad_cols + cols_came, ((0, 14), (0, 0))).astype(low_type)
    attend_low = jnp.concatenate([attend_low, cols_low])
    grad_group, contract_total, expand_pair, attend_low = meet(
        grad_group, contract_total, expand_pair, attend_low
    )
    shown_low = after((step_one + gate_two * branch_two).astype(low_type), grad_group)
    shown = from_latent(shown_low, chip, core)
    layer_out = latents_in + shown.astype(wide_type).reshape(latents_in.shape)
    shown_grad_low = after((back_two + back_one).astype(low_type), grad_group)
    shown_grad = from_latent(shown_grad_low, chip, core)
    latents_grad = cotangent + shown_grad.astype(wide_type).reshape(cotangent.shape)
    grad_all, layer_out, latents_grad, contract_came, expand_came, attend_first = meet(
        gather_groups(grad_group, group_count),
        layer_out,
        latents_grad,
        groups_third_came(contract_total, group_count),
        groups_second_came(expand_pair, group_count),
        groups_first_came(attend_low, group_count),
    )
    expand_total = groups_add(expand_pair, expand_came)
    attend_pair = groups_add(attend_low, attend_first)
    grad_all, contract_came, expand_total, attend_pair = meet(
        grad_all, contract_came, expand_total, attend_pair
    )
    rates = rates_table()
    grad_rows = jnp.sum(grad_all, 0, dtype=wide_type)
    grad_modulation_weight = jnp.einsum(
        "lc,lkr->ckr", silu_all, grad_all[:, :6], preferred_element_type=wide_type
    )
    state_modulation = adamw(
        modulation_weight, first_modulation, second_modulation, grad_modulation_weight, rates[0]
    )
    contract_third = groups_choose(contract_total, contract_came, group_count)
    contract_third = lax.optimization_barrier(contract_third.T)
    grad_contract_weight = contract_third.reshape(4, width_col, width_row).astype(wide_type)
    state_contract = adamw(
        contract_weight, first_contract, second_contract, grad_contract_weight, rates[4]
    )
    mark, mark_two, expand_came, attend_came = meet(
        state_modulation[0],
        state_contract[0],
        groups_third_came(expand_total, group_count),
        groups_second_came(attend_pair, group_count),
    )
    state_modulation = (mark,) + state_modulation[1:]
    state_contract = (mark_two,) + state_contract[1:]
    attend_total = groups_add(attend_pair, attend_came)
    attend_total, expand_came = meet(attend_total, expand_came)
    expand_third = groups_choose(expand_total, expand_came, group_count)
    expand_third = lax.optimization_barrier(expand_third.reshape(width_row, 4, width_col))
    grad_expand_weight = expand_third.astype(wide_type)
    state_expand = adamw(
        expand_weight, first_expand, second_expand, grad_expand_weight, rates[3]
    )
    silu_part = jnp.einsum(
        "lkr,ckr->lc",
        after(grad_group[:, :6], attend_total),
        modulation_low,
        preferred_element_type=wide_type,
    )
    grad_silu_order = sum_axis(silu_part, "row", 4).reshape(col_count, 4, width_col)
    grad_silu = jnp.stack(
        [
            lax.dynamic_index_in_dim(grad_silu_order, col_place ^ place, 0, False)
            for place in range(col_count)
        ]
    ).reshape(4 * col_count, width_col)
    mark, grad_silu, attend_came = meet(
        state_expand[0], grad_silu, groups_third_came(attend_total, group_count)
    )
    state_expand = (mark,) + state_expand[1:]
    attend_third = groups_choose(attend_total, attend_came, group_count)
    silu_value, silu_pull = jax.vjp(jax.nn.silu, conditioning)
    conditioning_grad = silu_pull(grad_silu)[0]

    cols_total = attend_third[width_row : width_row + 2].reshape(-1)[: 6 * width_col]
    cols_total = cols_total.reshape(6, width_col).astype(wide_type)
    grad_cols = jnp.concatenate([cols_total[4:], cols_total[:4]])
    attend_third = attend_third[:width_row]
    grad_attend_weight = jnp.stack(
        [
            attend_third[:, :width_col],
            attend_third[:, width_col : 2 * width_col],
            attend_third[:, 3 * width_col :],
        ]
    ).astype(wide_type)
    grad_output_weight = attend_third[:, 2 * width_col : 3 * width_col].T.astype(wide_type)
    states = [
        state_modulation,
        adamw(
            attention_in, first_attention_in, second_attention_in, grad_attend_weight, rates[1]
        ),
        adamw(
            attention_out, first_attention_out, second_attention_out, grad_output_weight, rates[2]
        ),
        state_expand,
        state_contract,
        adamw(bias_rows, first_bias_rows, second_bias_rows, grad_rows, rates[5]),
        adamw(bias_cols, first_bias_cols, second_bias_cols, grad_cols, rates[6]),
    ]
    return tuple(
        [layer_out, latents_grad, conditioning_grad]
        + [states[member][0] for member in range(7)]
        + [states[member][1] for member in range(7)]
        + [states[member][2] for member in range(7)]
    )


def solution(mesh):
    token_spec = P(("dp", "col"), "row")
    state_specs = (
        P("col", None, "row"),
        P(None, "row", "col"),
        P("col", "row"),
        P("row", None, "col"),
        P(None, "col", "row"),
        P(None, "row"),
        P(None, "col"),
    )
    in_specs = (token_spec, P("dp", "col"), token_spec) + state_specs * 3
    out_specs = (token_spec, token_spec, P("dp", "col")) + state_specs * 3

    def body(*arrays):
        return on_device(mesh.shape["dp"], mesh.shape["col"], *arrays)

    return jax.shard_map(
        body, mesh=mesh, in_specs=in_specs, out_specs=out_specs, check_vma=False
    )
```

```python
import math

import jax
import jax.numpy as jnp
from jax import lax
from jax.sharding import PartitionSpec as P

D = 1152
HD = 72
FF = 4608
SEQ = 256
STEP = 10


norm_eps = 1e-06
beta_first = 0.9
beta_second = 0.999
adam_eps = 1e-08
weight_decay = 0.01

low_type = jnp.bfloat16
wide_type = jnp.float32


def rates_table():
    base_rate = 1.5 / math.sqrt(D)
    return (base_rate, base_rate, 4.0 * base_rate, base_rate, 1.5 / math.sqrt(FF), 0.45, 0.45)


def adamw(weight, first_old, second, gradient, learn_rate):
    first_new = beta_first * first_old + (1.0 - beta_first) * gradient
    second_new = beta_second * second + (1.0 - beta_second) * gradient * gradient
    first_hat = first_new / (1.0 - beta_first**STEP)
    second_hat = second_new / (1.0 - beta_second**STEP)
    weight_new = weight - learn_rate * (
        first_hat / (jnp.sqrt(second_hat) + adam_eps) + weight_decay * weight
    )
    return (weight_new, first_new, second_new)


def matmul(left_side, right_side):
    return jnp.dot(left_side, right_side, preferred_element_type=wide_type)


def matmul_nt(left_side, right_side):
    return lax.dot_general(
        left_side, right_side, (((1,), (1,)), ((), ())), preferred_element_type=wide_type
    )


def matmul_tn(left_side, right_side):
    return lax.dot_general(
        left_side, right_side, (((0,), (0,)), ((), ())), preferred_element_type=wide_type
    )


def swap(tensor, axis, size, bit):
    return lax.ppermute(tensor, axis, [(place, place ^ bit) for place in range(size)])


def row_swap(tensor, bit):
    return swap(tensor, "row", 4, bit)


def after(tensor, *others):
    return lax.optimization_barrier((tensor,) + others)[0]


def meet(*tensors):
    return lax.optimization_barrier(tensors)


def gather_cores(shard, came):
    chips = jnp.concatenate([shard, came], 0)
    return jnp.concatenate([chips, row_swap(chips, 1)], 0)


def width_halves(left_side, right_side):
    half = left_side.shape[1] // 2
    sent = matmul_tn(left_side[:, half:], right_side).astype(low_type)
    return (matmul_tn(left_side[:, :half], right_side), sent)


def latent_parts(blocks, chip):
    pairs = blocks.reshape((2, 2) + blocks.shape[1:])
    kept = lax.dynamic_index_in_dim(pairs, chip, 0, False)
    return (kept, lax.dynamic_index_in_dim(pairs, 1 - chip, 0, False))


def latent_cores(chips, core):
    both = jnp.stack(chips)
    kept = lax.dynamic_index_in_dim(both, core, 1, False)
    came = row_swap(lax.dynamic_index_in_dim(both, 1 - core, 1, False), 1)
    return jnp.concatenate([kept[0], kept[1], came[0], came[1]], -1)


def from_latent(whole, chip, core):
    width = whole.shape[-1] // 4
    parts = [whole[:, place * width : (place + 1) * width] for place in range(4)]
    other = row_swap(jnp.stack(parts[2:]), 1)
    mine = jnp.stack([parts[0], other[0]])
    far = row_swap(jnp.stack([parts[1], other[1]]), 2)
    pairs = jnp.stack([mine, far])
    pairs = jnp.where(core == 1, pairs[:, ::-1], pairs)
    pairs = jnp.where(chip == 1, pairs[::-1], pairs)
    return pairs.reshape((4,) + pairs.shape[2:])


def gather_axis(tensor, axis, size):
    bit = 1
    while bit < size:
        tensor = jnp.concatenate([tensor, swap(tensor, axis, size, bit)], 0)
        bit *= 2
    return tensor


def gather_groups(tensor, size):
    return jnp.concatenate(
        [tensor] + [swap(tensor, "dp", size, place) for place in range(1, size)], 0
    )


def scatter_product(multiply, left_side, size):
    half = left_side.shape[0] // 2
    if size == 2:
        sent = multiply(left_side[half:]).astype(low_type)
        return (multiply(left_side[:half]), swap(sent, "col", size, 1))
    partial = multiply(left_side)
    bit = size // 2
    while bit > 1:
        half = partial.shape[0] // 2
        came = swap(partial[half:].astype(low_type), "col", size, bit)
        partial = partial[:half] + came.astype(wide_type)
        bit //= 2
    half = partial.shape[0] // 2
    return (partial[:half], swap(partial[half:].astype(low_type), "col", size, 1))


def sum_axis(tensor, axis, size):
    bit = 1
    while bit < size:
        tensor = tensor + swap(tensor, axis, size, bit)
        bit *= 2
    return tensor


def chips_parts(partial):
    half = partial.shape[0] // 2
    return (partial[:half], partial[half:].astype(low_type))


def groups_first_came(sent, size):
    if size != 4:
        return jnp.zeros_like(sent)
    return lax.ppermute(sent, "dp", [(0, 1), (3, 2)])


def groups_second_came(pair, size):
    if size != 4:
        return (lax.psum(pair, "dp").astype(wide_type) - pair.astype(wide_type)).astype(low_type)
    return lax.ppermute(pair, "dp", [(1, 2), (2, 1)])


def groups_third_came(total, size):
    if size != 4:
        return total
    return lax.ppermute(total, "dp", [(1, 0), (2, 3)])


def groups_add(kept, came):
    return (kept.astype(wide_type) + came.astype(wide_type)).astype(low_type)


def groups_choose(total, came, size):
    place = lax.axis_index("dp")
    return jnp.where((place == 1) | (place == 2) | (size != 4), total, came)


def normalize(stream):
    center = jnp.mean(stream, -1, keepdims=True)
    spread = jnp.mean(stream * stream, -1, keepdims=True) - center * center
    inverse = lax.rsqrt(spread + norm_eps)
    return ((stream - center) * inverse, inverse)


def normalize_back(grad_normed, normed, inverse):
    mean = jnp.mean(grad_normed, -1, keepdims=True)
    cross = jnp.mean(grad_normed * normed, -1, keepdims=True)
    return inverse * (grad_normed - mean - normed * cross)


def attention_forward(queries, key_rows, values):
    token_count, width = queries.shape
    shaped = (token_count // SEQ, SEQ, width // HD, HD)
    score_scale = 1.0 / math.sqrt(HD)
    scores = (
        jnp.einsum(
            "lqhe,lkhe->lhqk",
            queries.reshape(shaped),
            key_rows.reshape(shaped),
            preferred_element_type=wide_type,
        )
        * score_scale
    )
    row_max = jnp.max(scores, -1, keepdims=True)
    exponent = jnp.exp(scores - row_max)
    totals = jnp.sum(exponent, -1, keepdims=True)
    soft_weights = (exponent / totals).astype(low_type)
    attended = jnp.einsum(
        "lhqk,lkhe->lqhe", soft_weights, values.reshape(shaped), preferred_element_type=wide_type
    )
    return (attended.reshape(token_count, width).astype(low_type), row_max + jnp.log(totals))


def attention_backward(queries, key_rows, values, log_total, grad_attended):
    token_count, width = queries.shape
    shaped = (token_count // SEQ, SEQ, width // HD, HD)
    score_scale = 1.0 / math.sqrt(HD)
    query_heads = queries.reshape(shaped)
    key_heads = key_rows.reshape(shaped)
    value_heads = values.reshape(shaped)
    grad_heads = grad_attended.reshape(shaped)
    scores = (
        jnp.einsum("lqhe,lkhe->lhqk", query_heads, key_heads, preferred_element_type=wide_type)
        * score_scale
    )
    soft_float = jnp.exp(scores - log_total)
    grad_soft = jnp.einsum(
        "lqhe,lkhe->lhqk", grad_heads, value_heads, preferred_element_type=wide_type
    )
    grad_values = jnp.einsum(
        "lhqk,lqhe->lkhe",
        soft_float.astype(low_type),
        grad_heads,
        preferred_element_type=wide_type,
    )
    inner = jnp.sum(soft_float * grad_soft, -1, keepdims=True)
    grad_scores = (soft_float * (grad_soft - inner)).astype(low_type)
    grad_queries = (
        jnp.einsum("lhqk,lkhe->lqhe", grad_scores, key_heads, preferred_element_type=wide_type)
        * score_scale
    )
    grad_keys = (
        jnp.einsum("lhqk,lqhe->lkhe", grad_scores, query_heads, preferred_element_type=wide_type)
        * score_scale
    )
    joined = jnp.concatenate(
        [
            grad_queries.reshape(token_count, width),
            grad_keys.reshape(token_count, width),
            grad_values.reshape(token_count, width),
        ],
        1,
    )
    return joined.astype(low_type)


def on_device(
    group_count,
    col_count,
    latents_in,
    conditioning,
    cotangent,
    modulation_weight,
    attention_in,
    attention_out,
    expand_weight,
    contract_weight,
    bias_rows,
    bias_cols,
    first_modulation,
    first_attention_in,
    first_attention_out,
    first_expand,
    first_contract,
    first_bias_rows,
    first_bias_cols,
    second_modulation,
    second_attention_in,
    second_attention_out,
    second_expand,
    second_contract,
    second_bias_rows,
    second_bias_cols,
):
    width_row = latents_in.shape[1]
    width_col = attention_in.shape[2]
    row_place = lax.axis_index("row")
    chip, core = row_place // 2, row_place % 2
    col_place = lax.axis_index("col")

    stream_parts = latent_parts(latents_in.astype(low_type).reshape(4, SEQ, width_row), chip)
    conditioning_first = after(conditioning, stream_parts[1])
    silu_low = jax.nn.silu(conditioning_first).astype(low_type)
    modulation_low = modulation_weight.astype(low_type)
    modulation_part = jnp.einsum(
        "lc,ckr->lkr", silu_low, modulation_low, preferred_element_type=wide_type
    ).reshape(col_count, 4, 6, width_row)
    if col_count == 2:
        kept = lax.dynamic_index_in_dim(modulation_part, col_place, 0, False)
        sent = lax.dynamic_index_in_dim(modulation_part, 1 - col_place, 0, False)
        modulation_row = kept + swap(sent, "col", 2, 1)
    else:
        modulation_row = lax.psum_scatter(modulation_part, "col", scatter_dimension=0)
    modulation_row = jnp.concatenate(
        [modulation_row + bias_rows[:6], jnp.broadcast_to(bias_rows[6:], (4, 2, width_row))], 1
    )
    modulation_parts = latent_parts(modulation_row, chip)
    attend_shard = jnp.concatenate([attention_in[part].astype(low_type) for part in range(3)], 1)
    stream_came, modulation_came, attend_shard = meet(
        row_swap(stream_parts[1], 2), row_swap(modulation_parts[1], 2), attend_shard
    )
    modulation = latent_cores((modulation_parts[0], modulation_came), core)
    shift_one, scale_one, gate_one, shift_two, scale_two, gate_two, bias_out, bias_contract = [
        modulation[member : member + 1] for member in range(8)
    ]
    stream = latent_cores((stream_parts[0], stream_came), core).astype(wide_type)

    normed_one, inverse_one = normalize(stream)
    act_one = (normed_one * (1.0 + scale_one) + shift_one).astype(low_type)
    cotangent_late, output_late, expand_late, contract_late, act_one = meet(
        cotangent, attention_out, expand_weight, contract_weight, act_one
    )
    cotangent_parts = latent_parts(
        cotangent_late.astype(low_type).reshape(4, SEQ, width_row), chip
    )
    output_shard = output_late.astype(low_type).T
    expand_shard = expand_late.astype(low_type).reshape(width_row, 4 * width_col)
    contract_shard = contract_late.astype(low_type)
    contract_shard = contract_shard.reshape(4 * width_col, width_row).T
    act_one_all, attend_came, cotangent_sent, output_shard, expand_shard, contract_shard = meet(
        gather_axis(act_one, "col", col_count),
        row_swap(attend_shard, 2),
        cotangent_parts[1],
        output_shard,
        expand_shard,
        contract_shard,
    )
    attend_matrix = gather_cores(attend_shard, attend_came)
    attend_sums = matmul(act_one_all, attend_matrix)
    queries = (attend_sums[:, :width_col] + bias_cols[0]).astype(low_type)
    key_rows = attend_sums[:, width_col : 2 * width_col].astype(low_type)
    values = (attend_sums[:, 2 * width_col :] + bias_cols[1]).astype(low_type)
    queries, contract_shard = meet(queries, contract_shard)
    attended, log_total = attention_forward(queries, key_rows, values)
    attended, output_came, cotangent_came = meet(
        attended, row_swap(output_shard, 2), row_swap(cotangent_sent, 2)
    )
    silu_order = jnp.stack(
        [
            lax.dynamic_index_in_dim(
                silu_low.reshape(col_count, 4, width_col), col_place ^ place, 0, False
            )
            for place in range(col_count)
        ]
    )
    output_matrix = gather_cores(output_shard, output_came)
    stream_grad = latent_cores((cotangent_parts[0], cotangent_came), core).astype(wide_type)
    grad_branch_two = (gate_two * stream_grad).astype(low_type)
    branch_one_own, branch_one_came = scatter_product(
        lambda left_side: matmul_nt(left_side, output_matrix), attended, col_count
    )
    branch_one_own, expand_came, grad_branch_two_all = meet(
        branch_one_own,
        row_swap(expand_shard, 2),
        gather_axis(grad_branch_two, "col", col_count),
    )
    expand_matrix = gather_cores(expand_shard, expand_came)
    branch_one_own, branch_one_came, contract_came = meet(
        branch_one_own, branch_one_came, row_swap(contract_shard, 2)
    )
    branch_one = branch_one_own + branch_one_came.astype(wide_type) + bias_out
    step_one = gate_one * branch_one
    middle = stream + step_one
    normed_two, inverse_two = normalize(middle)
    act_two = (normed_two * (1.0 + scale_two) + shift_two).astype(low_type)
    silu_group = after(silu_order.reshape(4 * col_count, width_col), act_two)
    contract_matrix = gather_cores(contract_shard, contract_came)
    act_two_all, expand_matrix, silu_all = meet(
        gather_axis(act_two, "col", col_count),
        expand_matrix,
        gather_groups(silu_group, group_count),
    )
    hidden_pre = matmul(act_two_all, expand_matrix) + bias_cols[2:6].reshape(-1)
    hidden, gelu_pull = jax.vjp(lambda value: jax.nn.gelu(value, approximate=True), hidden_pre)
    hidden = hidden.astype(low_type)

    grad_hidden_act = matmul(grad_branch_two_all, contract_matrix)
    grad_hidden = gelu_pull(grad_hidden_act)[0].astype(low_type)
    grad_act_two_own, grad_act_two_came = scatter_product(
        lambda left_side: matmul_nt(left_side, expand_matrix), grad_hidden, col_count
    )
    hidden, grad_act_two_own = meet(hidden, grad_act_two_own)
    contract_kept, contract_sent = width_halves(grad_branch_two_all, hidden)
    branch_two_own, branch_two_came = scatter_product(
        lambda left_side: matmul_nt(left_side, contract_matrix),
        after(hidden, contract_sent),
        col_count,
    )
    grad_act_two_own, grad_act_two_came, contract_kept, contract_came, branch_two_own = meet(
        grad_act_two_own,
        grad_act_two_came,
        contract_kept,
        row_swap(contract_sent, 1),
        branch_two_own,
    )
    grad_act_two = grad_act_two_own + grad_act_two_came.astype(wide_type)
    contract_parts = chips_parts(contract_kept + contract_came.astype(wide_type))
    grad_act_two, contract_sent = meet(grad_act_two, contract_parts[1])
    grad_shift_two = jnp.sum(grad_act_two, 0)
    grad_scale_two = jnp.sum(grad_act_two * normed_two, 0)
    back_two = normalize_back(grad_act_two * (1.0 + scale_two), normed_two, inverse_two)
    grad_middle = stream_grad + back_two
    grad_gate_one = jnp.sum(grad_middle * branch_one, 0)

    grad_branch_one = (gate_one * grad_middle).astype(low_type)
    expand_kept, expand_sent = width_halves(after(act_two_all, grad_branch_one), grad_hidden)
    grad_branch_one_all, expand_kept, expand_came = meet(
        gather_axis(grad_branch_one, "col", col_count),
        expand_kept,
        row_swap(expand_sent, 1),
    )
    grad_attended = matmul(grad_branch_one_all, output_matrix).astype(low_type)
    expand_parts = chips_parts(expand_kept + expand_came.astype(wide_type))
    grad_attended, expand_sent = meet(grad_attended, expand_parts[1])
    grad_attend = attention_backward(queries, key_rows, values, log_total, grad_attended)
    grad_attend, contract_came = meet(grad_attend, row_swap(contract_sent, 2))
    contract_low = (contract_parts[0] + contract_came.astype(wide_type)).astype(low_type)
    grad_attend, contract_low = meet(grad_attend, contract_low)
    grad_act_one_own, grad_act_one_came = scatter_product(
        lambda left_side: matmul_nt(left_side, attend_matrix), grad_attend, col_count
    )
    attend_all, grad_branch_one_all, grad_act_one_own = meet(
        grad_attend, grad_branch_one_all, grad_act_one_own
    )
    halves = [
        width_halves(act_one_all, attend_all[:, : 2 * width_col]),
        width_halves(grad_branch_one_all, attended),
        width_halves(act_one_all, attend_all[:, 2 * width_col :]),
    ]
    grad_cols = jnp.concatenate(
        [
            jnp.sum(grad_hidden, 0, dtype=wide_type),
            jnp.sum(attend_all[:, :width_col], 0, dtype=wide_type),
            jnp.sum(attend_all[:, 2 * width_col :], 0, dtype=wide_type),
            jnp.zeros((2 * width_col,), wide_type),
        ]
    ).reshape(2, 4 * width_col)
    grad_act_one_own, grad_act_one_came, branch_two_came, expand_came, contract_first, *pieces = meet(
        grad_act_one_own,
        grad_act_one_came,
        branch_two_came,
        row_swap(expand_sent, 2),
        groups_first_came(contract_low, group_count),
        *[kept for kept, _ in halves],
        *[row_swap(sent, 1) for _, sent in halves],
    )
    attend_parts = [
        chips_parts(kept + came.astype(wide_type)) for kept, came in zip(pieces[:3], pieces[3:])
    ]
    attend_sent = jnp.concatenate([sent for _, sent in attend_parts], 1)
    expand_low = (expand_parts[0] + expand_came.astype(wide_type)).astype(low_type)
    contract_pair = groups_add(contract_low, contract_first)
    contract_pair, expand_low, attend_sent, grad_act_one_own = meet(
        contract_pair, expand_low, attend_sent, grad_act_one_own
    )
    branch_two = branch_two_own + branch_two_came.astype(wide_type) + bias_contract
    grad_gate_two = jnp.sum(stream_grad * branch_two, 0)
    grad_act_one = grad_act_one_own + grad_act_one_came.astype(wide_type)
    grad_shift_one = jnp.sum(grad_act_one, 0)
    grad_scale_one = jnp.sum(grad_act_one * normed_one, 0)
    back_one = normalize_back(grad_act_one * (1.0 + scale_one), normed_one, inverse_one)

    grad_own = jnp.stack(
        [
            grad_shift_one,
            grad_scale_one,
            grad_gate_one,
            grad_shift_two,
            grad_scale_two,
            grad_gate_two,
            jnp.sum(grad_branch_one, 0, dtype=wide_type),
            jnp.sum(grad_branch_two, 0, dtype=wide_type),
        ]
    ).astype(low_type)
    grad_cols = grad_cols + row_swap(grad_cols, 1)
    attend_kept = jnp.concatenate([kept.astype(low_type) for kept, _ in attend_parts], 1)
    grad_own, contract_came, expand_first, attend_came, cols_came, attend_kept = meet(
        grad_own,
        groups_second_came(contract_pair, group_count),
        groups_first_came(expand_low, group_count),
        row_swap(attend_sent, 2),
        row_swap(grad_cols, 2),
        attend_kept,
    )
    attend_low = groups_add(attend_kept, attend_came)
    cols_low = jnp.pad(grad_cols + cols_came, ((0, 14), (0, 0))).astype(low_type)
    attend_low = jnp.concatenate([attend_low, cols_low])
    attend_low, contract_came, expand_first = meet(attend_low, contract_came, expand_first)
    contract_total = groups_add(contract_pair, contract_came)
    expand_pair = groups_add(expand_low, expand_first)
    grad_own, contract_total, expand_pair, attend_low = meet(
        grad_own, contract_total, expand_pair, attend_low
    )
    grad_row = from_latent(grad_own, chip, core)
    grad_group = gather_axis(grad_row[None], "col", col_count)
    grad_group = grad_group.reshape(4 * col_count, 8, width_row)
    shown_low = after((step_one + gate_two * branch_two).astype(low_type), grad_own)
    shown = from_latent(shown_low, chip, core)
    layer_out = latents_in + shown.astype(wide_type).reshape(latents_in.shape)
    layer_out, grad_group, contract_came, expand_came, attend_first = meet(
        layer_out,
        grad_group,
        groups_third_came(contract_total, group_count),
        groups_second_came(expand_pair, group_count),
        groups_first_came(attend_low, group_count),
    )
    attend_pair = groups_add(attend_low, attend_first)
    attend_pair, contract_came, expand_came = meet(attend_pair, contract_came, expand_came)
    expand_total = groups_add(expand_pair, expand_came)
    expand_total, contract_came, grad_group = meet(expand_total, contract_came, grad_group)
    shown_grad_low = after((back_two + back_one).astype(low_type), contract_came)
    shown_grad = from_latent(shown_grad_low, chip, core)
    latents_grad = cotangent + shown_grad.astype(wide_type).reshape(cotangent.shape)
    rates = rates_table()
    contract_third = groups_choose(contract_total, contract_came, group_count)
    contract_third = lax.optimization_barrier(contract_third.T)
    grad_contract_weight = contract_third.reshape(4, width_col, width_row).astype(wide_type)
    state_contract = adamw(
        contract_weight, first_contract, second_contract, grad_contract_weight, rates[4]
    )
    mark, latents_grad, grad_all, expand_came, attend_came = meet(
        state_contract[0],
        latents_grad,
        gather_groups(grad_group, group_count),
        groups_third_came(expand_total, group_count),
        groups_second_came(attend_pair, group_count),
    )
    state_contract = (mark,) + state_contract[1:]
    attend_total = groups_add(attend_pair, attend_came)
    attend_total, expand_came, grad_all = meet(attend_total, expand_came, grad_all)
    grad_rows = jnp.sum(grad_all, 0, dtype=wide_type)
    grad_modulation_weight = jnp.einsum(
        "lc,lkr->ckr", silu_all, grad_all[:, :6], preferred_element_type=wide_type
    )
    state_modulation = adamw(
        modulation_weight, first_modulation, second_modulation, grad_modulation_weight, rates[0]
    )
    expand_third = groups_choose(expand_total, expand_came, group_count)
    expand_third = lax.optimization_barrier(expand_third.reshape(width_row, 4, width_col))
    grad_expand_weight = expand_third.astype(wide_type)
    state_expand = adamw(
        expand_weight, first_expand, second_expand, grad_expand_weight, rates[3]
    )
    silu_part = jnp.einsum(
        "lkr,ckr->lc",
        after(grad_group[:, :6], attend_total),
        modulation_low,
        preferred_element_type=wide_type,
    )
    grad_silu_order = sum_axis(silu_part, "row", 4).reshape(col_count, 4, width_col)
    grad_silu = jnp.stack(
        [
            lax.dynamic_index_in_dim(grad_silu_order, col_place ^ place, 0, False)
            for place in range(col_count)
        ]
    ).reshape(4 * col_count, width_col)
    mark, mark_two, grad_silu, attend_came = meet(
        state_expand[0],
        state_modulation[0],
        grad_silu,
        groups_third_came(attend_total, group_count),
    )
    state_expand = (mark,) + state_expand[1:]
    state_modulation = (mark_two,) + state_modulation[1:]
    attend_third = groups_choose(attend_total, attend_came, group_count)
    silu_value, silu_pull = jax.vjp(jax.nn.silu, conditioning)
    conditioning_grad = silu_pull(grad_silu)[0]

    cols_total = attend_third[width_row : width_row + 2].reshape(-1)[: 6 * width_col]
    cols_total = cols_total.reshape(6, width_col).astype(wide_type)
    grad_cols = jnp.concatenate([cols_total[4:], cols_total[:4]])
    attend_third = attend_third[:width_row]
    grad_attend_weight = jnp.stack(
        [
            attend_third[:, :width_col],
            attend_third[:, width_col : 2 * width_col],
            attend_third[:, 3 * width_col :],
        ]
    ).astype(wide_type)
    grad_output_weight = attend_third[:, 2 * width_col : 3 * width_col].T.astype(wide_type)
    states = [
        state_modulation,
        adamw(
            attention_in, first_attention_in, second_attention_in, grad_attend_weight, rates[1]
        ),
        adamw(
            attention_out, first_attention_out, second_attention_out, grad_output_weight, rates[2]
        ),
        state_expand,
        state_contract,
        adamw(bias_rows, first_bias_rows, second_bias_rows, grad_rows, rates[5]),
        adamw(bias_cols, first_bias_cols, second_bias_cols, grad_cols, rates[6]),
    ]
    return tuple(
        [layer_out, latents_grad, conditioning_grad]
        + [states[member][0] for member in range(7)]
        + [states[member][1] for member in range(7)]
        + [states[member][2] for member in range(7)]
    )


def solution(mesh):
    token_spec = P(("dp", "col"), "row")
    state_specs = (
        P("col", None, "row"),
        P(None, "row", "col"),
        P("col", "row"),
        P("row", None, "col"),
        P(None, "col", "row"),
        P(None, "row"),
        P(None, "col"),
    )
    in_specs = (token_spec, P("dp", "col"), token_spec) + state_specs * 3
    out_specs = (token_spec, token_spec, P("dp", "col")) + state_specs * 3

    def body(*arrays):
        return on_device(mesh.shape["dp"], mesh.shape["col"], *arrays)

    return jax.shard_map(
        body, mesh=mesh, in_specs=in_specs, out_specs=out_specs, check_vma=False
    )
```

```python
import math

import jax
import jax.numpy as jnp
from jax import lax
from jax.sharding import PartitionSpec as P

D = 1152
HD = 72
FF = 4608
SEQ = 256
STEP = 10


norm_eps = 1e-06
beta_first = 0.9
beta_second = 0.999
adam_eps = 1e-08
weight_decay = 0.01

low_type = jnp.bfloat16
wide_type = jnp.float32


def rates_table():
    base_rate = 1.5 / math.sqrt(D)
    return (base_rate, base_rate, 4.0 * base_rate, base_rate, 1.5 / math.sqrt(FF), 0.45, 0.45)


def adamw(weight, first_old, second, gradient, learn_rate):
    first_new = beta_first * first_old + (1.0 - beta_first) * gradient
    second_new = beta_second * second + (1.0 - beta_second) * gradient * gradient
    first_hat = first_new / (1.0 - beta_first**STEP)
    second_hat = second_new / (1.0 - beta_second**STEP)
    weight_new = weight - learn_rate * (
        first_hat / (jnp.sqrt(second_hat) + adam_eps) + weight_decay * weight
    )
    return (weight_new, first_new, second_new)


def matmul(left_side, right_side):
    return jnp.dot(left_side, right_side, preferred_element_type=wide_type)


def matmul_nt(left_side, right_side):
    return lax.dot_general(
        left_side, right_side, (((1,), (1,)), ((), ())), preferred_element_type=wide_type
    )


def matmul_tn(left_side, right_side):
    return lax.dot_general(
        left_side, right_side, (((0,), (0,)), ((), ())), preferred_element_type=wide_type
    )


def swap(tensor, axis, size, bit):
    return lax.ppermute(tensor, axis, [(place, place ^ bit) for place in range(size)])


def row_swap(tensor, bit):
    return swap(tensor, "row", 4, bit)


def after(tensor, *others):
    return lax.optimization_barrier((tensor,) + others)[0]


def meet(*tensors):
    return lax.optimization_barrier(tensors)


def gather_cores(shard, came):
    chips = jnp.concatenate([shard, came], 0)
    return jnp.concatenate([chips, row_swap(chips, 1)], 0)


def width_halves(left_side, right_side):
    half = left_side.shape[1] // 2
    sent = matmul_tn(left_side[:, half:], right_side).astype(low_type)
    return (matmul_tn(left_side[:, :half], right_side), sent)


def latent_parts(blocks, chip):
    pairs = blocks.reshape((2, 2) + blocks.shape[1:])
    kept = lax.dynamic_index_in_dim(pairs, chip, 0, False)
    return (kept, lax.dynamic_index_in_dim(pairs, 1 - chip, 0, False))


def latent_cores(chips, core):
    both = jnp.stack(chips)
    kept = lax.dynamic_index_in_dim(both, core, 1, False)
    came = row_swap(lax.dynamic_index_in_dim(both, 1 - core, 1, False), 1)
    return jnp.concatenate([kept[0], kept[1], came[0], came[1]], -1)


def from_latent(whole, chip, core):
    width = whole.shape[-1] // 4
    parts = [whole[:, place * width : (place + 1) * width] for place in range(4)]
    other = row_swap(jnp.stack(parts[2:]), 1)
    mine = jnp.stack([parts[0], other[0]])
    far = row_swap(jnp.stack([parts[1], other[1]]), 2)
    pairs = jnp.stack([mine, far])
    pairs = jnp.where(core == 1, pairs[:, ::-1], pairs)
    pairs = jnp.where(chip == 1, pairs[::-1], pairs)
    return pairs.reshape((4,) + pairs.shape[2:])


def gather_axis(tensor, axis, size):
    bit = 1
    while bit < size:
        tensor = jnp.concatenate([tensor, swap(tensor, axis, size, bit)], 0)
        bit *= 2
    return tensor


def gather_groups(tensor, size):
    return jnp.concatenate(
        [tensor] + [swap(tensor, "dp", size, place) for place in range(1, size)], 0
    )


def scatter_product(multiply, left_side, size):
    half = left_side.shape[0] // 2
    if size == 2:
        sent = multiply(left_side[half:]).astype(low_type)
        return (multiply(left_side[:half]), swap(sent, "col", size, 1))
    partial = multiply(left_side)
    bit = size // 2
    while bit > 1:
        half = partial.shape[0] // 2
        came = swap(partial[half:].astype(low_type), "col", size, bit)
        partial = partial[:half] + came.astype(wide_type)
        bit //= 2
    half = partial.shape[0] // 2
    return (partial[:half], swap(partial[half:].astype(low_type), "col", size, 1))


def sum_axis(tensor, axis, size):
    bit = 1
    while bit < size:
        tensor = tensor + swap(tensor, axis, size, bit)
        bit *= 2
    return tensor


def chips_parts(partial):
    half = partial.shape[0] // 2
    return (partial[:half], partial[half:].astype(low_type))


def groups_first_came(sent, size):
    if size != 4:
        return jnp.zeros_like(sent)
    return lax.ppermute(sent, "dp", [(0, 1), (3, 2)])


def groups_second_came(pair, size):
    if size != 4:
        return (lax.psum(pair, "dp").astype(wide_type) - pair.astype(wide_type)).astype(low_type)
    return lax.ppermute(pair, "dp", [(1, 2), (2, 1)])


def groups_third_came(total, size):
    if size != 4:
        return total
    return lax.ppermute(total, "dp", [(1, 0), (2, 3)])


def groups_add(kept, came):
    return (kept.astype(wide_type) + came.astype(wide_type)).astype(low_type)


def groups_choose(total, came, size):
    place = lax.axis_index("dp")
    return jnp.where((place == 1) | (place == 2) | (size != 4), total, came)


def normalize(stream):
    center = jnp.mean(stream, -1, keepdims=True)
    spread = jnp.mean(stream * stream, -1, keepdims=True) - center * center
    inverse = lax.rsqrt(spread + norm_eps)
    return ((stream - center) * inverse, inverse)


def normalize_back(grad_normed, normed, inverse):
    mean = jnp.mean(grad_normed, -1, keepdims=True)
    cross = jnp.mean(grad_normed * normed, -1, keepdims=True)
    return inverse * (grad_normed - mean - normed * cross)


def attention_forward(queries, key_rows, values):
    token_count, width = queries.shape
    shaped = (token_count // SEQ, SEQ, width // HD, HD)
    score_scale = 1.0 / math.sqrt(HD)
    scores = (
        jnp.einsum(
            "lqhe,lkhe->lhqk",
            queries.reshape(shaped),
            key_rows.reshape(shaped),
            preferred_element_type=wide_type,
        )
        * score_scale
    )
    row_max = jnp.max(scores, -1, keepdims=True)
    values, row_max = meet(values, row_max)
    exponent = jnp.exp(scores - row_max)
    totals = jnp.sum(exponent, -1, keepdims=True)
    soft_weights = (exponent / totals).astype(low_type)
    attended = jnp.einsum(
        "lhqk,lkhe->lqhe", soft_weights, values.reshape(shaped), preferred_element_type=wide_type
    )
    return (attended.reshape(token_count, width).astype(low_type), row_max + jnp.log(totals))


def attention_backward(queries, key_rows, values, log_total, grad_attended):
    token_count, width = queries.shape
    shaped = (token_count // SEQ, SEQ, width // HD, HD)
    score_scale = 1.0 / math.sqrt(HD)
    query_heads = queries.reshape(shaped)
    key_heads = key_rows.reshape(shaped)
    value_heads = values.reshape(shaped)
    grad_heads = grad_attended.reshape(shaped)
    scores = (
        jnp.einsum("lqhe,lkhe->lhqk", query_heads, key_heads, preferred_element_type=wide_type)
        * score_scale
    )
    soft_float = jnp.exp(scores - log_total)
    grad_soft = jnp.einsum(
        "lqhe,lkhe->lhqk", grad_heads, value_heads, preferred_element_type=wide_type
    )
    grad_values = jnp.einsum(
        "lhqk,lqhe->lkhe",
        soft_float.astype(low_type),
        grad_heads,
        preferred_element_type=wide_type,
    )
    inner = jnp.sum(soft_float * grad_soft, -1, keepdims=True)
    grad_scores = (soft_float * (grad_soft - inner)).astype(low_type)
    grad_queries = (
        jnp.einsum("lhqk,lkhe->lqhe", grad_scores, key_heads, preferred_element_type=wide_type)
        * score_scale
    )
    grad_keys = (
        jnp.einsum("lhqk,lqhe->lkhe", grad_scores, query_heads, preferred_element_type=wide_type)
        * score_scale
    )
    joined = jnp.concatenate(
        [
            grad_queries.reshape(token_count, width),
            grad_keys.reshape(token_count, width),
            grad_values.reshape(token_count, width),
        ],
        1,
    )
    return joined.astype(low_type)


def on_device(
    group_count,
    col_count,
    latents_in,
    conditioning,
    cotangent,
    modulation_weight,
    attention_in,
    attention_out,
    expand_weight,
    contract_weight,
    bias_rows,
    bias_cols,
    first_modulation,
    first_attention_in,
    first_attention_out,
    first_expand,
    first_contract,
    first_bias_rows,
    first_bias_cols,
    second_modulation,
    second_attention_in,
    second_attention_out,
    second_expand,
    second_contract,
    second_bias_rows,
    second_bias_cols,
):
    width_row = latents_in.shape[1]
    width_col = attention_in.shape[2]
    row_place = lax.axis_index("row")
    chip, core = row_place // 2, row_place % 2
    col_place = lax.axis_index("col")

    stream_parts = latent_parts(latents_in.astype(low_type).reshape(4, SEQ, width_row), chip)
    conditioning_first = after(conditioning, stream_parts[1])
    silu_low = jax.nn.silu(conditioning_first).astype(low_type)
    modulation_low = modulation_weight.astype(low_type)
    modulation_part = jnp.einsum(
        "lc,ckr->lkr", silu_low, modulation_low, preferred_element_type=wide_type
    ).reshape(col_count, 4, 6, width_row)
    if col_count == 2:
        kept = lax.dynamic_index_in_dim(modulation_part, col_place, 0, False)
        sent = lax.dynamic_index_in_dim(modulation_part, 1 - col_place, 0, False)
        modulation_row = kept + swap(sent, "col", 2, 1)
    else:
        modulation_row = lax.psum_scatter(modulation_part, "col", scatter_dimension=0)
    modulation_row = jnp.concatenate(
        [modulation_row + bias_rows[:6], jnp.broadcast_to(bias_rows[6:], (4, 2, width_row))], 1
    )
    modulation_parts = latent_parts(modulation_row, chip)
    attend_shard = jnp.concatenate([attention_in[part].astype(low_type) for part in range(3)], 1)
    stream_came, modulation_came, attend_shard = meet(
        row_swap(stream_parts[1], 2), row_swap(modulation_parts[1], 2), attend_shard
    )
    modulation = latent_cores((modulation_parts[0], modulation_came), core)
    shift_one, scale_one, gate_one, shift_two, scale_two, gate_two, bias_out, bias_contract = [
        modulation[member : member + 1] for member in range(8)
    ]
    stream = latent_cores((stream_parts[0], stream_came), core).astype(wide_type)

    normed_one, inverse_one = normalize(stream)
    act_one = (normed_one * (1.0 + scale_one) + shift_one).astype(low_type)
    cotangent_late, output_late, expand_late, contract_late, act_one = meet(
        cotangent, attention_out, expand_weight, contract_weight, act_one
    )
    cotangent_parts = latent_parts(
        cotangent_late.astype(low_type).reshape(4, SEQ, width_row), chip
    )
    output_shard = output_late.astype(low_type).T
    expand_shard = expand_late.astype(low_type).reshape(width_row, 4 * width_col)
    contract_shard = contract_late.astype(low_type)
    contract_shard = contract_shard.reshape(4 * width_col, width_row).T
    act_one_all, attend_came, cotangent_sent, output_shard, expand_shard, contract_shard = meet(
        gather_axis(act_one, "col", col_count),
        row_swap(attend_shard, 2),
        cotangent_parts[1],
        output_shard,
        expand_shard,
        contract_shard,
    )
    attend_matrix = gather_cores(attend_shard, attend_came)
    attend_sums = matmul(act_one_all, attend_matrix)
    queries = (attend_sums[:, :width_col] + bias_cols[0]).astype(low_type)
    key_rows = attend_sums[:, width_col : 2 * width_col].astype(low_type)
    values = (attend_sums[:, 2 * width_col :] + bias_cols[1]).astype(low_type)
    queries, contract_shard = meet(queries, contract_shard)
    attended, log_total = attention_forward(queries, key_rows, values)
    attended, output_came, cotangent_came = meet(
        attended, row_swap(output_shard, 2), row_swap(cotangent_sent, 2)
    )
    silu_order = jnp.stack(
        [
            lax.dynamic_index_in_dim(
                silu_low.reshape(col_count, 4, width_col), col_place ^ place, 0, False
            )
            for place in range(col_count)
        ]
    )
    output_matrix = gather_cores(output_shard, output_came)
    stream_grad = latent_cores((cotangent_parts[0], cotangent_came), core).astype(wide_type)
    grad_branch_two = (gate_two * stream_grad).astype(low_type)
    branch_one_own, branch_one_came = scatter_product(
        lambda left_side: matmul_nt(left_side, output_matrix), attended, col_count
    )
    branch_one_own, expand_came, grad_branch_two_all = meet(
        branch_one_own,
        row_swap(expand_shard, 2),
        gather_axis(grad_branch_two, "col", col_count),
    )
    expand_matrix = gather_cores(expand_shard, expand_came)
    branch_one_own, branch_one_came, contract_came = meet(
        branch_one_own, branch_one_came, row_swap(contract_shard, 2)
    )
    branch_one = branch_one_own + branch_one_came.astype(wide_type) + bias_out
    step_one = gate_one * branch_one
    middle = stream + step_one
    normed_two, inverse_two = normalize(middle)
    act_two = (normed_two * (1.0 + scale_two) + shift_two).astype(low_type)
    silu_group = after(silu_order.reshape(4 * col_count, width_col), act_two)
    contract_matrix = gather_cores(contract_shard, contract_came)
    act_two_all, expand_matrix, silu_all = meet(
        gather_axis(act_two, "col", col_count),
        expand_matrix,
        gather_groups(silu_group, group_count),
    )
    hidden_pre = matmul(act_two_all, expand_matrix) + bias_cols[2:6].reshape(-1)
    hidden, gelu_pull = jax.vjp(lambda value: jax.nn.gelu(value, approximate=True), hidden_pre)
    hidden = hidden.astype(low_type)

    grad_hidden_act = matmul(grad_branch_two_all, contract_matrix)
    grad_hidden = gelu_pull(grad_hidden_act)[0].astype(low_type)
    grad_act_two_own, grad_act_two_came = scatter_product(
        lambda left_side: matmul_nt(left_side, expand_matrix), grad_hidden, col_count
    )
    hidden, grad_act_two_own = meet(hidden, grad_act_two_own)
    contract_kept, contract_sent = width_halves(grad_branch_two_all, hidden)
    branch_two_own, branch_two_came = scatter_product(
        lambda left_side: matmul_nt(left_side, contract_matrix),
        after(hidden, contract_sent),
        col_count,
    )
    grad_act_two_own, grad_act_two_came, contract_kept, contract_came, branch_two_own = meet(
        grad_act_two_own,
        grad_act_two_came,
        contract_kept,
        row_swap(contract_sent, 1),
        branch_two_own,
    )
    grad_act_two = grad_act_two_own + grad_act_two_came.astype(wide_type)
    contract_parts = chips_parts(contract_kept + contract_came.astype(wide_type))
    grad_act_two, contract_sent = meet(grad_act_two, contract_parts[1])
    grad_shift_two = jnp.sum(grad_act_two, 0)
    grad_scale_two = jnp.sum(grad_act_two * normed_two, 0)
    back_two = normalize_back(grad_act_two * (1.0 + scale_two), normed_two, inverse_two)
    grad_middle = stream_grad + back_two
    grad_gate_one = jnp.sum(grad_middle * branch_one, 0)

    grad_branch_one = (gate_one * grad_middle).astype(low_type)
    expand_kept, expand_sent = width_halves(after(act_two_all, grad_branch_one), grad_hidden)
    grad_branch_one_all, expand_kept, expand_came = meet(
        gather_axis(grad_branch_one, "col", col_count),
        expand_kept,
        row_swap(expand_sent, 1),
    )
    grad_attended = matmul(grad_branch_one_all, output_matrix).astype(low_type)
    expand_parts = chips_parts(expand_kept + expand_came.astype(wide_type))
    grad_attended, expand_sent = meet(grad_attended, expand_parts[1])
    grad_attend = attention_backward(queries, key_rows, values, log_total, grad_attended)
    grad_attend, contract_came = meet(grad_attend, row_swap(contract_sent, 2))
    contract_low = (contract_parts[0] + contract_came.astype(wide_type)).astype(low_type)
    grad_attend, contract_low = meet(grad_attend, contract_low)
    grad_act_one_own, grad_act_one_came = scatter_product(
        lambda left_side: matmul_nt(left_side, attend_matrix), grad_attend, col_count
    )
    attend_all, grad_branch_one_all, grad_act_one_own = meet(
        grad_attend, grad_branch_one_all, grad_act_one_own
    )
    halves = [
        width_halves(act_one_all, attend_all[:, : 2 * width_col]),
        width_halves(grad_branch_one_all, attended),
        width_halves(act_one_all, attend_all[:, 2 * width_col :]),
    ]
    grad_cols = jnp.concatenate(
        [
            jnp.sum(grad_hidden, 0, dtype=wide_type),
            jnp.sum(attend_all[:, :width_col], 0, dtype=wide_type),
            jnp.sum(attend_all[:, 2 * width_col :], 0, dtype=wide_type),
            jnp.zeros((2 * width_col,), wide_type),
        ]
    ).reshape(2, 4 * width_col)
    grad_act_one_own, grad_act_one_came, branch_two_came, expand_came, contract_first, *pieces = meet(
        grad_act_one_own,
        grad_act_one_came,
        branch_two_came,
        row_swap(expand_sent, 2),
        groups_first_came(contract_low, group_count),
        *[kept for kept, _ in halves],
        *[row_swap(sent, 1) for _, sent in halves],
    )
    attend_parts = [
        chips_parts(kept + came.astype(wide_type)) for kept, came in zip(pieces[:3], pieces[3:])
    ]
    attend_sent = jnp.concatenate([sent for _, sent in attend_parts], 1)
    expand_low = (expand_parts[0] + expand_came.astype(wide_type)).astype(low_type)
    contract_pair = groups_add(contract_low, contract_first)
    contract_pair, expand_low, attend_sent, grad_act_one_own = meet(
        contract_pair, expand_low, attend_sent, grad_act_one_own
    )
    branch_two = branch_two_own + branch_two_came.astype(wide_type) + bias_contract
    grad_gate_two = jnp.sum(stream_grad * branch_two, 0)
    grad_act_one = grad_act_one_own + grad_act_one_came.astype(wide_type)
    grad_shift_one = jnp.sum(grad_act_one, 0)
    grad_scale_one = jnp.sum(grad_act_one * normed_one, 0)
    back_one = normalize_back(grad_act_one * (1.0 + scale_one), normed_one, inverse_one)

    grad_own = jnp.stack(
        [
            grad_shift_one,
            grad_scale_one,
            grad_gate_one,
            grad_shift_two,
            grad_scale_two,
            grad_gate_two,
            jnp.sum(grad_branch_one, 0, dtype=wide_type),
            jnp.sum(grad_branch_two, 0, dtype=wide_type),
        ]
    ).astype(low_type)
    grad_cols = grad_cols + row_swap(grad_cols, 1)
    attend_kept = jnp.concatenate([kept.astype(low_type) for kept, _ in attend_parts], 1)
    grad_own, contract_came, expand_first, attend_came, cols_came, attend_kept = meet(
        grad_own,
        groups_second_came(contract_pair, group_count),
        groups_first_came(expand_low, group_count),
        row_swap(attend_sent, 2),
        row_swap(grad_cols, 2),
        attend_kept,
    )
    attend_low = groups_add(attend_kept, attend_came)
    cols_low = jnp.pad(grad_cols + cols_came, ((0, 14), (0, 0))).astype(low_type)
    attend_low = jnp.concatenate([attend_low, cols_low])
    attend_low, contract_came, expand_first = meet(attend_low, contract_came, expand_first)
    contract_total = groups_add(contract_pair, contract_came)
    expand_pair = groups_add(expand_low, expand_first)
    grad_own, contract_total, expand_pair, attend_low = meet(
        grad_own, contract_total, expand_pair, attend_low
    )
    grad_row = from_latent(grad_own, chip, core)
    grad_group = gather_axis(grad_row[None], "col", col_count)
    grad_group = grad_group.reshape(4 * col_count, 8, width_row)
    shown_low = after((step_one + gate_two * branch_two).astype(low_type), grad_own)
    shown = from_latent(shown_low, chip, core)
    layer_out = latents_in + shown.astype(wide_type).reshape(latents_in.shape)
    layer_out, grad_group, contract_came, expand_came, attend_first = meet(
        layer_out,
        grad_group,
        groups_third_came(contract_total, group_count),
        groups_second_came(expand_pair, group_count),
        groups_first_came(attend_low, group_count),
    )
    attend_pair = groups_add(attend_low, attend_first)
    attend_pair, contract_came, expand_came = meet(attend_pair, contract_came, expand_came)
    expand_total = groups_add(expand_pair, expand_came)
    expand_total, contract_came, grad_group = meet(expand_total, contract_came, grad_group)
    shown_grad_low = after((back_two + back_one).astype(low_type), contract_came)
    shown_grad = from_latent(shown_grad_low, chip, core)
    latents_grad = cotangent + shown_grad.astype(wide_type).reshape(cotangent.shape)
    rates = rates_table()
    contract_third = groups_choose(contract_total, contract_came, group_count)
    contract_third = lax.optimization_barrier(contract_third.T)
    grad_contract_weight = contract_third.reshape(4, width_col, width_row).astype(wide_type)
    state_contract = adamw(
        contract_weight, first_contract, second_contract, grad_contract_weight, rates[4]
    )
    mark, latents_grad, grad_all, expand_came, attend_came = meet(
        state_contract[0],
        latents_grad,
        gather_groups(grad_group, group_count),
        groups_third_came(expand_total, group_count),
        groups_second_came(attend_pair, group_count),
    )
    state_contract = (mark,) + state_contract[1:]
    attend_total = groups_add(attend_pair, attend_came)
    attend_total, expand_came, grad_all = meet(attend_total, expand_came, grad_all)
    grad_rows = jnp.sum(grad_all, 0, dtype=wide_type)
    grad_modulation_weight = jnp.einsum(
        "lc,lkr->ckr", silu_all, grad_all[:, :6], preferred_element_type=wide_type
    )
    state_modulation = adamw(
        modulation_weight, first_modulation, second_modulation, grad_modulation_weight, rates[0]
    )
    expand_third = groups_choose(expand_total, expand_came, group_count)
    expand_third = lax.optimization_barrier(expand_third.reshape(width_row, 4, width_col))
    grad_expand_weight = expand_third.astype(wide_type)
    state_expand = adamw(
        expand_weight, first_expand, second_expand, grad_expand_weight, rates[3]
    )
    silu_part = jnp.einsum(
        "lkr,ckr->lc",
        after(grad_group[:, :6], attend_total),
        modulation_low,
        preferred_element_type=wide_type,
    )
    grad_silu_order = sum_axis(silu_part, "row", 4).reshape(col_count, 4, width_col)
    grad_silu = jnp.stack(
        [
            lax.dynamic_index_in_dim(grad_silu_order, col_place ^ place, 0, False)
            for place in range(col_count)
        ]
    ).reshape(4 * col_count, width_col)
    mark, mark_two, grad_silu, attend_came = meet(
        state_expand[0],
        state_modulation[0],
        grad_silu,
        groups_third_came(attend_total, group_count),
    )
    state_expand = (mark,) + state_expand[1:]
    state_modulation = (mark_two,) + state_modulation[1:]
    attend_third = groups_choose(attend_total, attend_came, group_count)
    silu_value, silu_pull = jax.vjp(jax.nn.silu, conditioning)
    conditioning_grad = silu_pull(grad_silu)[0]

    cols_total = attend_third[width_row : width_row + 2].reshape(-1)[: 6 * width_col]
    cols_total = cols_total.reshape(6, width_col).astype(wide_type)
    grad_cols = jnp.concatenate([cols_total[4:], cols_total[:4]])
    attend_third = attend_third[:width_row]
    grad_attend_weight = jnp.stack(
        [
            attend_third[:, :width_col],
            attend_third[:, width_col : 2 * width_col],
            attend_third[:, 3 * width_col :],
        ]
    ).astype(wide_type)
    grad_output_weight = attend_third[:, 2 * width_col : 3 * width_col].T.astype(wide_type)
    states = [
        state_modulation,
        adamw(
            attention_in, first_attention_in, second_attention_in, grad_attend_weight, rates[1]
        ),
        adamw(
            attention_out, first_attention_out, second_attention_out, grad_output_weight, rates[2]
        ),
        state_expand,
        state_contract,
        adamw(bias_rows, first_bias_rows, second_bias_rows, grad_rows, rates[5]),
        adamw(bias_cols, first_bias_cols, second_bias_cols, grad_cols, rates[6]),
    ]
    return tuple(
        [layer_out, latents_grad, conditioning_grad]
        + [states[member][0] for member in range(7)]
        + [states[member][1] for member in range(7)]
        + [states[member][2] for member in range(7)]
    )


def solution(mesh):
    token_spec = P(("dp", "col"), "row")
    state_specs = (
        P("col", None, "row"),
        P(None, "row", "col"),
        P("col", "row"),
        P("row", None, "col"),
        P(None, "col", "row"),
        P(None, "row"),
        P(None, "col"),
    )
    in_specs = (token_spec, P("dp", "col"), token_spec) + state_specs * 3
    out_specs = (token_spec, token_spec, P("dp", "col")) + state_specs * 3

    def body(*arrays):
        return on_device(mesh.shape["dp"], mesh.shape["col"], *arrays)

    return jax.shard_map(
        body, mesh=mesh, in_specs=in_specs, out_specs=out_specs, check_vma=False
    )
```
